256 devices in a mesh: seq: 32 (over z, x), head: 8 (over y, core).
Axes of the slice: x: 4, y: 4, z: 8, core: 2. Of those that a mesh axis runs over, the one named last changes fastest.
Arguments:
- queries: bfloat16 [32768, 2048], P('seq', 'head'), may hold values from -80 to 80
- keys: bfloat16 [32768, 2048], P('seq', 'head'), may hold values from -8 to 8
- values: bfloat16 [32768, 2048], P('seq', 'head'), may hold values from -6 to 6
- out_grad: bfloat16 [32768, 2048], P('seq', 'head'), may hold values from -6 to 6
- members: int32 [16, 32, 1024], P('head', 'seq'), may hold values from 0 to 32767, as said below
- centroids: float32 [16, 32, 128], P('head', 'seq'), may hold values from -6 to 6
- proj_weight: bfloat16 [3, 2048, 2048], P(None, None, 'head'), may hold values from -0.125 to 0.125
Outputs:
- input_grad: bfloat16 [32768, 2048], P('seq', 'head')
- new_centroids: float32 [16, 32, 128], P('head', 'seq')
The draws below stay inside these ranges and needn't reach their ends.
Inputs may be any that keep to these rules, and one draw needn't show every extreme that they name: members[h, c] holds 1024 token indices in increasing order; every token lies in exactly one cluster of each head; at most 64 of the tokens of one index of seq (rows k * 1024 to (k + 1) * 1024 - 1) lie in one cluster of one head, and in every head some cluster takes exactly 64 of them.
All inputs are finite; a program needn't handle non-finite values.
Results may differ from the reference program's by a relative error of at most 0.017.
Values may be sent and summed in bfloat16 or wider, within the bound.
A program may use at most 64 MiB of HBM per device.

```python
import math
import jax
import jax.numpy as jnp
from jax import lax

D = 2048
HEADS = 16
HD = 128
W = 1024
CLUSTERS = 32
TOK_DEV = 1024
TOKENS = 32768
N_SEQ = 32
N_HEAD = 8


def cluster_lists(key):
    base_key = jax.random.fold_in(key, 101)
    mean_size = W // N_SEQ
    cluster_total = CLUSTERS

    def one_head(head_key):
        size_key, order_key, label_key = jax.random.split(head_key, 3)
        halves = jax.random.randint(size_key, (N_SEQ // 2,), -mean_size, mean_size + 1).at[0].set(mean_size)
        run_sizes = jnp.stack([mean_size + halves, mean_size - halves], axis=1).reshape(N_SEQ)
        shuffled = jax.random.permutation(order_key, cluster_total)
        shifted = (shuffled[None, :] - jnp.arange(N_SEQ)[:, None]) % N_SEQ
        counts = run_sizes[shifted]
        run_ends = jnp.cumsum(counts, axis=1)
        places = jnp.arange(TOK_DEV)

        def per_device(device_key, row_ends):
            labels = jnp.sum((places[:, None] >= row_ends[None, :]).astype(jnp.int32), axis=1)
            return jax.random.permutation(device_key, labels)
        labels = jax.vmap(per_device)(jax.random.split(label_key, N_SEQ), run_ends).reshape(TOKENS)
        scores = labels * TOKENS + jnp.arange(TOKENS)
        return jnp.argsort(scores, stable=True).reshape(cluster_total, W).astype(jnp.int32)
    return jax.vmap(one_head)(jax.random.split(base_key, HEADS))


def draw_members(key, part):
    return cluster_lists(key)


def draw_keys(key, part):
    key = jax.random.fold_in(key, 11)
    return jnp.clip(jax.random.normal(key, (TOKENS, HEADS * HD)), -6.0, 6.0).astype(jnp.bfloat16)


def draw_queries(key, part):
    key = jax.random.fold_in(key, 12)
    return jnp.clip(jax.random.normal(key, (TOKENS, HEADS * HD)), -6.0, 6.0).astype(jnp.bfloat16)


def steps_of(stream_key, extent, cuts, least, top_value):
    factor_of = 1.0
    for axis_at, shards_of in cuts:
        heights = jax.random.uniform(jax.random.fold_in(jax.random.fold_in(stream_key, 6), axis_at), (shards_of,), jnp.float32, least / len(cuts), top_value / len(cuts))
        factor_of = factor_of * jnp.repeat(jnp.exp(heights), extent[axis_at] // shards_of).reshape((-1,) + (1,) * (len(extent) - 1 - axis_at))
    return factor_of


def noise(key, dims, width, most, cuts=(), dtype=jnp.bfloat16):
    level = steps_of(key, dims, cuts, -0.22, 0.18) if cuts else 1.0
    result = jax.random.normal(key, dims, jnp.float32) * width * level
    return jnp.minimum(jnp.maximum(result, -most), most).astype(dtype)


def setup_inputs(seed: int = 0) -> dict:
    seeds = jax.random.split(jax.random.key(seed), 8)
    return {
        "queries": draw_queries(jax.random.fold_in(seeds[7], 71), 0),
        "keys": draw_keys(jax.random.fold_in(seeds[7], 71), 0),
        "values": noise(seeds[2], (TOKENS, HEADS * HD), 1.0, 6.0, ((0, 32), (1, 8))),
        "out_grad": noise(seeds[3], (TOKENS, HEADS * HD), 1.0, 6.0, ((0, 32), (1, 8))),
        "members": draw_members(jax.random.fold_in(seeds[7], 71), 0),
        "centroids": noise(seeds[5], (HEADS, CLUSTERS, HD), 1.0, 6.0, ((0, 8), (1, 32)), jnp.float32),
        "proj_weight": noise(seeds[6], (3, D, HEADS * HD), D ** -0.5, 0.125, ((2, 8),)),
    }


decay_rate = 0.99

def cluster_backward(query_rows, key_rows, value_rows, grad_rows):
    cluster_width, head_width = query_rows.shape
    score_scale = 1.0 / math.sqrt(head_width)
    block_rows = min(512, cluster_width)
    key_total = jnp.zeros((cluster_width, head_width), jnp.float32)
    value_total = jnp.zeros((cluster_width, head_width), jnp.float32)
    pieces = []
    for block_pos in range(cluster_width // block_rows):
        row_low = block_pos * block_rows
        row_high = row_low + block_rows
        query_block = query_rows[row_low:row_high]
        grad_block = grad_rows[row_low:row_high]
        key_prefix = key_rows[:row_high]
        value_prefix = value_rows[:row_high]
        scores = lax.dot_general(query_block, key_prefix, (((1,), (1,)), ((), ())), preferred_element_type=jnp.float32) * score_scale
        causal = jnp.arange(row_high)[None, :] <= (row_low + jnp.arange(block_rows))[:, None]
        scores = jnp.where(causal, scores, -jnp.inf)
        attn_probs = jax.nn.softmax(scores, axis=-1)
        probs_low = attn_probs.astype(jnp.bfloat16)
        output = jnp.dot(probs_low, value_prefix, preferred_element_type=jnp.float32)
        row_delta = lax.optimization_barrier(jnp.sum(grad_block.astype(jnp.float32) * output, axis=1, keepdims=True))
        prob_grad = lax.dot_general(grad_block, value_prefix, (((1,), (1,)), ((), ())), preferred_element_type=jnp.float32)
        score_grad = (attn_probs * (prob_grad - row_delta)).astype(jnp.bfloat16)
        pieces.append((jnp.dot(score_grad, key_prefix, preferred_element_type=jnp.float32) * score_scale).astype(jnp.bfloat16))
        key_total = key_total.at[:row_high].add(lax.dot_general(score_grad, query_block, (((0,), (0,)), ((), ())), preferred_element_type=jnp.float32))
        value_total = value_total.at[:row_high].add(lax.dot_general(probs_low, grad_block, (((0,), (0,)), ((), ())), preferred_element_type=jnp.float32))
    return (jnp.concatenate(pieces, axis=0), (key_total * score_scale).astype(jnp.bfloat16), value_total.astype(jnp.bfloat16))

def reference(queries, keys, values, out_grad, members, centroids, proj_weight):
    token_count, columns = queries.shape
    head_count = members.shape[0]
    head_width = columns // head_count

    def one_head(head_pos):
        member_rows = members[head_pos]
        start_col = (head_pos * head_width).astype(jnp.int32)
        query_head = lax.dynamic_slice_in_dim(queries, start_col, head_width, axis=1)[member_rows]
        key_head = lax.dynamic_slice_in_dim(keys, start_col, head_width, axis=1)[member_rows]
        value_head = lax.dynamic_slice_in_dim(values, start_col, head_width, axis=1)[member_rows]
        grad_head = lax.dynamic_slice_in_dim(out_grad, start_col, head_width, axis=1)[member_rows]

        def one_cluster(rows):
            return cluster_backward(rows[0], rows[1], rows[2], rows[3])
        query_grad, key_grad, value_grad = lax.map(one_cluster, (query_head, key_head, value_head, grad_head))
        stacked = jnp.stack([query_grad, key_grad, value_grad], axis=2).reshape(-1, 3, head_width)
        grad_rows = jnp.zeros((token_count, 3, head_width), jnp.bfloat16).at[member_rows.reshape(-1)].set(stacked)
        key_sums = lax.optimization_barrier(jnp.sum(query_head.astype(jnp.float32), axis=1)) + lax.optimization_barrier(jnp.sum(key_head.astype(jnp.float32), axis=1))
        moved_cent = decay_rate * centroids[head_pos] + 0.5 * (1.0 - decay_rate) * key_sums
        return (grad_rows, moved_cent)
    grad_rows, new_centroids = lax.map(one_head, jnp.arange(head_count).astype(jnp.int32))
    per_group = head_count // N_HEAD
    grad_total = jnp.zeros((token_count, proj_weight.shape[1]), jnp.float32)
    for group_pos in range(N_HEAD):
        group_part = jnp.zeros((token_count, proj_weight.shape[1]), jnp.float32)
        col_low = group_pos * per_group * head_width
        col_high = col_low + per_group * head_width
        for which in range(3):
            chosen = grad_rows[group_pos * per_group:(group_pos + 1) * per_group, :, which, :]
            chosen = jnp.transpose(chosen, (1, 0, 2)).reshape(token_count, per_group * head_width)
            weight_cols = proj_weight[which][:, col_low:col_high]
            group_part = group_part + lax.dot_general(chosen, weight_cols, (((1,), (1,)), ((), ())), preferred_element_type=jnp.float32)
        grad_total = grad_total + lax.optimization_barrier(group_part.astype(jnp.bfloat16)).astype(jnp.float32)
    return (grad_total.astype(jnp.bfloat16), new_centroids)
```

```python
import math

import jax
import jax.numpy as jnp
from jax import lax
from jax.experimental import pallas as pl
from jax.experimental.pallas import tpu as pltpu
from jax.sharding import PartitionSpec as P

MESH = pl.DeviceIdType.MESH
F32 = jnp.float32
BF16 = jnp.bfloat16

decay_rate = 0.99

N = 32
NZ, NX = 8, 4
NY = 4
TOK = 1024
W = 1024
CAP = 64
HD = 128
HEADS = 2
SLOTS = N * CAP
GROUP = 4
BLK = 256
RC = 8
RROWS = TOK // RC
SELF_STEP = (NZ - 1) * NX


def one_hot(mask):
    return jnp.where(mask, 1.0, 0.0).astype(BF16)


def iota(shape, dim):
    return lax.broadcasted_iota(jnp.int32, shape, dim).astype(F32)


def dot_nt(a, b):
    return lax.dot_general(a, b, (((1,), (1,)), ((), ())), preferred_element_type=F32)


def dot_nn(a, b):
    return jnp.dot(a, b, preferred_element_type=F32)


def kernel(
    q_ref, k_ref, v_ref, g_ref, mem_ref, cent_ref, w_ref,
    out_ref, newc_ref,
    tab, codes_s, codes_r, destrow, dest_t, slot_t, hot,
    stage_f, recv_f, x_ref, y_ref, dk_ref, dv_ref, p_scr, d_scr, k_t,
    stage_r, recv_r, z_ref, part, part_r, p2, hop_r, hop_s, dir_r, last_r,
    code_ss, code_rs, fwd_ss, fwd_rs, ret_ss, ret_rs, self_sem,
    core_ss, core_rs, hop_ss, hop_rs, dir_ss, dir_rs, last_ss, last_rs,
):
    me = lax.axis_index("seq")
    hd = lax.axis_index("head")
    my_z, my_x = lax.div(me, NX), lax.rem(me, NX)
    my_y, core = lax.div(hd, 2), lax.rem(hd, 2)
    sibling = my_y * 2 + (1 - core)
    y_next = lax.rem(my_y + 1, NY)
    y_prev = lax.rem(my_y + NY - 1, NY)
    y_far = lax.rem(my_y + 2, NY)
    next_hd = y_next * 2 + core
    prev_hd = y_prev * 2 + core

    def peer(n):
        step = lax.div(n, NX)
        dx = lax.rem(n, NX)
        half = lax.div(step, 2)
        odd = lax.rem(step, 2)
        dz = jnp.where(step == NZ - 1, 0, jnp.where(odd == 1, NZ - 1 - half, 1 + half))
        return lax.rem(my_z + dz, NZ) * NX + lax.rem(my_x + dx, NX)

    barrier = pltpu.get_barrier_semaphore()

    def greet(n, carry):
        @pl.when(n != SELF_STEP)
        def _():
            pl.semaphore_signal(barrier, inc=1, device_id=(peer(n), hd), device_id_type=MESH)
        return carry

    lax.fori_loop(0, N, greet, 0)
    for other in (sibling, next_hd, prev_hd):
        pl.semaphore_signal(barrier, inc=1, device_id=(me, other), device_id_type=MESH)

    for h in range(HEADS):
        m = mem_ref[h]
        hi = m >> 10
        lo = m & (TOK - 1)
        dev = lax.broadcasted_iota(jnp.int32, (N, W), 0)
        eq = hi == dev
        start = jnp.sum(jnp.where(hi < dev, 1.0, 0.0), axis=1, keepdims=True)
        count = jnp.sum(jnp.where(eq, 1.0, 0.0), axis=1, keepdims=True)
        start_of = jnp.sum(jnp.where(eq, start, 0.0), axis=0, keepdims=True)
        rank = iota((1, W), 1) + 1.0 - start_of
        ranks = jnp.where(eq, rank, 0.0).astype(BF16)
        for tb in range(TOK // BLK):
            tok = lax.broadcasted_iota(jnp.int32, (BLK, W), 0) + tb * BLK
            codes = dot_nt(ranks, one_hot(lo == tok))
            for part_at in range(BLK // 128):
                codes_s[:, h, tb * (BLK // 128) + part_at, :] = codes[
                    :, part_at * 128 : (part_at + 1) * 128
                ]
        slot = lax.broadcasted_iota(jnp.int32, (N, SLOTS), 1)
        dev2 = lax.broadcasted_iota(jnp.int32, (N, SLOTS), 0)
        rank_at = (slot & (CAP - 1)).astype(F32)
        place = jnp.where(rank_at < count, start + rank_at, -1.0)
        dest = jnp.sum(jnp.where((slot >> 6) == dev2, place, 0.0), axis=0, keepdims=True)
        destrow[h] = dest
        dest_t[h] = jnp.transpose(jnp.broadcast_to(dest, (128, SLOTS)))

    pl.semaphore_wait(barrier, N - 1 + 3)

    def code_copy(n, src_at, dst_at, other):
        return pltpu.make_async_remote_copy(
            src_ref=codes_s.at[src_at], dst_ref=codes_r.at[dst_at],
            send_sem=code_ss.at[n], recv_sem=code_rs.at[dst_at],
            device_id=(other, hd), device_id_type=MESH,
        )

    def send_codes(n, carry):
        @pl.when(n != SELF_STEP)
        def _():
            to = peer(n)
            code_copy(n, to, me, to).start()
        return carry

    lax.fori_loop(0, N, send_codes, 0)
    codes_r[me] = codes_s[me]
    for h in range(HEADS):
        for at, ref in enumerate((q_ref, k_ref, v_ref, g_ref)):
            tab[h, :, at * HD : (at + 1) * HD] = ref[:, h * HD : (h + 1) * HD]

    def wait_codes(n, carry):
        @pl.when(n != SELF_STEP)
        def _():
            src = peer(n)
            code_copy(n, src, src, src).wait_recv()
        return carry

    lax.fori_loop(0, N, wait_codes, 0)

    def fwd_copy(h, n, dst_at, other):
        return pltpu.make_async_remote_copy(
            src_ref=stage_f.at[h, n], dst_ref=recv_f.at[h, dst_at],
            send_sem=fwd_ss.at[h, n], recv_sem=fwd_rs.at[h, dst_at],
            device_id=(other, hd), device_id_type=MESH,
        )

    def ret_copy(h, n, dst_at, other):
        return pltpu.make_async_remote_copy(
            src_ref=stage_r.at[h, n], dst_ref=recv_r.at[h, dst_at],
            send_sem=ret_ss.at[h, n], recv_sem=ret_rs.at[h, dst_at],
            device_id=(other, hd), device_id_type=MESH,
        )

    def fwd_self(h):
        return pltpu.make_async_copy(stage_f.at[h, SELF_STEP], recv_f.at[h, me], self_sem.at[0, h])

    def ret_self(h):
        return pltpu.make_async_copy(stage_r.at[h, SELF_STEP], recv_r.at[h, me], self_sem.at[1, h])

    def launch(h, gi, copy_of, self_of):
        for u in range(GROUP):
            n = gi * GROUP + u
            to = peer(n)

            @pl.when(n != SELF_STEP)
            def _():
                copy_of(h, n, me, to).start()

            @pl.when(n == SELF_STEP)
            def _():
                self_of(h).start()

    def wait_all(h, copy_of, self_of):
        def one(n, carry):
            @pl.when(n != SELF_STEP)
            def _():
                src = peer(n)
                copy_of(h, n, src, src).wait_recv()
            return carry

        lax.fori_loop(0, N, one, 0)
        self_of(h).wait()

    rank_rows = iota((CAP, 128), 0) + 1.0
    lanes = iota((CAP, 128), 1)

    def gather_head(h, carry):
        def group(gi, inner):
            for u in range(GROUP):
                to = peer(gi * GROUP + u)
                for tc in range(TOK // 128):
                    row = codes_r[to, h, tc : tc + 1, :]
                    hot[u * CAP : (u + 1) * CAP, tc * 128 : (tc + 1) * 128] = one_hot(row == rank_rows)
            rows = dot_nn(hot[:, :TOK], tab[h])
            stage_f[h, pl.ds(gi * GROUP, GROUP)] = rows.astype(BF16).reshape(GROUP, CAP, 4 * HD)
            launch(h, gi, fwd_copy, fwd_self)
            return inner

        return lax.fori_loop(0, N // GROUP, group, carry)

    lax.fori_loop(0, HEADS, gather_head, 0)

    for h in range(HEADS):
        slot = jnp.zeros((TOK // 128, 128), F32)
        for c in range(N):
            code = codes_r[c, h]
            slot = slot + jnp.where(code > 0.0, code + (c * CAP - 1.0), 0.0)
        for tc in range(TOK // 128):
            slot_t[h, tc * 128 : (tc + 1) * 128, :] = jnp.transpose(
                jnp.broadcast_to(slot[tc : tc + 1, :], (128, 128))
            )

    exp_scale = math.log2(math.e) / math.sqrt(HD)
    scale = 1.0 / math.sqrt(HD)
    causal = lax.broadcasted_iota(jnp.int32, (BLK, BLK), 0) <= lax.broadcasted_iota(
        jnp.int32, (BLK, BLK), 1
    )

    def cluster_head(h, carry):
        wait_all(h, fwd_copy, fwd_self)

        def order(ib, sums):
            place = iota((BLK, 128), 0) + (ib * BLK).astype(F32)
            for pc in range(SLOTS // 128):
                row = destrow[h, :, pc * 128 : (pc + 1) * 128]
                hot[:, pc * 128 : (pc + 1) * 128] = one_hot(row == place)
            rows = dot_nn(hot[...], recv_f[h].reshape(SLOTS, 4 * HD))
            x_ref[pl.ds(ib * BLK, BLK), :] = rows.astype(BF16)
            return sums + jnp.sum(rows[:, :HD] + rows[:, HD : 2 * HD], axis=0, keepdims=True)

        sums = lax.fori_loop(0, W // BLK, order, jnp.zeros((1, HD), F32))
        newc_ref[h] = decay_rate * cent_ref[h] + 0.5 * (1.0 - decay_rate) * sums

        k_t[...] = jnp.transpose(x_ref[:, HD : 2 * HD].astype(F32)).astype(BF16)

        for b in range(W // BLK):
            low = b * BLK
            q_b = x_ref[low : low + BLK, 0:HD]
            g_b = x_ref[low : low + BLK, 3 * HD : 4 * HD]
            top = None
            for jb in range(b + 1):
                s = dot_nt(x_ref[jb * BLK : (jb + 1) * BLK, HD : 2 * HD], q_b)
                if jb == b:
                    s = jnp.where(causal, s, -jnp.inf)
                p_scr[jb] = s
                part_top = jnp.max(s, axis=0, keepdims=True)
                top = part_top if top is None else jnp.maximum(top, part_top)
            total = jnp.zeros((1, BLK), F32)
            delta = jnp.zeros((1, BLK), F32)
            for jb in range(b + 1):
                p = jnp.exp2((p_scr[jb] - top) * exp_scale)
                d = dot_nt(x_ref[jb * BLK : (jb + 1) * BLK, 2 * HD : 3 * HD], g_b)
                p_scr[jb] = p
                d_scr[jb] = d
                total = total + jnp.sum(p, axis=0, keepdims=True)
                delta = delta + jnp.sum(p * d, axis=0, keepdims=True)
            inv = 1.0 / total
            delta = delta * inv
            dq_t = jnp.zeros((HD, BLK), F32)
            for jb in range(b + 1):
                rows = slice(jb * BLK, (jb + 1) * BLK)
                p = p_scr[jb] * inv
                p_low = p.astype(BF16)
                ds = (p * (d_scr[jb] - delta)).astype(BF16)
                dv = dot_nn(p_low, g_b)
                dk = dot_nn(ds, q_b)
                dq_t = dq_t + dot_nn(k_t[:, rows], ds)
                if jb == b:
                    dv_ref[rows, :] = dv
                    dk_ref[rows, :] = dk
                else:
                    dv_ref[rows, :] += dv
                    dk_ref[rows, :] += dk
            y_ref[low : low + BLK, 0:HD] = (jnp.transpose(dq_t) * scale).astype(BF16)
        y_ref[:, HD : 2 * HD] = (dk_ref[...] * scale).astype(BF16)
        y_ref[:, 2 * HD : 3 * HD] = dv_ref[...].astype(BF16)

        def group(gi, inner):
            for u in range(GROUP):
                to = peer(gi * GROUP + u)
                place = dest_t[h, pl.ds(pl.multiple_of(to * CAP, CAP), CAP), :]
                for ic in range(W // 128):
                    hot[u * CAP : (u + 1) * CAP, ic * 128 : (ic + 1) * 128] = one_hot(
                        place == lanes + ic * 128.0
                    )
            rows = dot_nn(hot[:, :W], y_ref[...])
            stage_r[h, pl.ds(gi * GROUP, GROUP)] = rows.astype(BF16).reshape(GROUP, CAP, 3 * HD)
            launch(h, gi, ret_copy, ret_self)
            return inner

        return lax.fori_loop(0, N // GROUP, group, carry)

    lax.fori_loop(0, HEADS, cluster_head, 0)

    def tokens(h, tb):
        wide = iota((BLK, 128), 1)
        rows_at = pl.ds(pl.multiple_of(tb * BLK, BLK), BLK)
        place = slot_t[h, rows_at, :]
        for pc in range(SLOTS // 128):
            hot[:, pc * 128 : (pc + 1) * 128] = one_hot(place == wide + pc * 128.0)
        rows = dot_nn(hot[...], recv_r[h].reshape(SLOTS, 3 * HD)).astype(BF16)
        for a in range(3):
            at = a * HEADS * HD + h * HD
            z_ref[rows_at, at : at + HD] = rows[:, a * HD : (a + 1) * HD]

    wait_all(0, ret_copy, ret_self)
    lax.fori_loop(0, TOK // BLK, lambda tb, c: (tokens(0, tb), c)[1], 0)
    wait_all(1, ret_copy, ret_self)

    def core_copy(rc):
        return pltpu.make_async_remote_copy(
            src_ref=part.at[rc, 1 - core], dst_ref=part_r.at[rc],
            send_sem=core_ss.at[rc], recv_sem=core_rs.at[rc],
            device_id=(me, sibling), device_id_type=MESH,
        )

    def hop_copy(rc):
        return pltpu.make_async_remote_copy(
            src_ref=p2.at[rc, y_far], dst_ref=hop_r.at[rc],
            send_sem=hop_ss.at[rc], recv_sem=hop_rs.at[rc],
            device_id=(me, next_hd if rc % 2 == 0 else prev_hd), device_id_type=MESH,
        )

    def dir_copy(rc):
        return pltpu.make_async_remote_copy(
            src_ref=p2.at[rc, y_prev if rc % 2 == 0 else y_next], dst_ref=dir_r.at[rc],
            send_sem=dir_ss.at[rc], recv_sem=dir_rs.at[rc],
            device_id=(me, prev_hd if rc % 2 == 0 else next_hd), device_id_type=MESH,
        )

    def last_copy(rc):
        return pltpu.make_async_remote_copy(
            src_ref=hop_s.at[rc], dst_ref=last_r.at[rc],
            send_sem=last_ss.at[rc], recv_sem=last_rs.at[rc],
            device_id=(me, next_hd if rc % 2 == 0 else prev_hd), device_id_type=MESH,
        )

    def project(tb):
        tokens(1, tb)
        z = z_ref[tb * BLK : (tb + 1) * BLK, :]

        def one(d, carry):
            acc = None
            for a in range(3):
                term = dot_nt(
                    z[:, a * HEADS * HD : (a + 1) * HEADS * HD],
                    w_ref[a, pl.ds(pl.multiple_of(d * 256, 256), 256), :],
                )
                acc = term if acc is None else acc + term
            low = acc.astype(BF16)
            for piece in range(BLK // RROWS):
                part[tb * (BLK // RROWS) + piece, lax.rem(d, 2), lax.div(d, 2)] = low[
                    piece * RROWS : (piece + 1) * RROWS
                ]
            return carry

        lax.fori_loop(0, 2 * NY, one, 0)

    def merge(rc):
        core_copy(rc).wait_recv()
        p2[rc] = (part[rc, core].astype(F32) + part_r[rc].astype(F32)).astype(BF16)
        hop_copy(rc).start()
        dir_copy(rc).start()

    def relay(rc):
        hop_copy(rc).wait_recv()
        mine = p2[rc, y_next if rc % 2 == 0 else y_prev]
        hop_s[rc] = (hop_r[rc].astype(F32) + mine.astype(F32)).astype(BF16)
        last_copy(rc).start()

    def finish(rc):
        dir_copy(rc).wait_recv()
        last_copy(rc).wait_recv()
        total = p2[rc, my_y].astype(F32) + dir_r[rc].astype(F32) + last_r[rc].astype(F32)
        out_ref[rc * RROWS : (rc + 1) * RROWS, :] = total.astype(BF16)

    per = BLK // RROWS
    for step in range(TOK // BLK + 3):
        if step < TOK // BLK:
            project(step)
            for rc in range(step * per, (step + 1) * per):
                core_copy(rc).start()
        if 1 <= step <= TOK // BLK:
            for rc in range((step - 1) * per, step * per):
                merge(rc)
        if 2 <= step <= TOK // BLK + 1:
            for rc in range((step - 2) * per, (step - 1) * per):
                relay(rc)
    for rc in range(RC):
        finish(rc)

    def drain(n, carry):
        @pl.when(n != SELF_STEP)
        def _():
            to = peer(n)
            code_copy(n, to, me, to).wait_send()
            for h in range(HEADS):
                fwd_copy(h, n, me, to).wait_send()
                ret_copy(h, n, me, to).wait_send()
        return carry

    lax.fori_loop(0, N, drain, 0)
    for rc in range(RC):
        core_copy(rc).wait_send()
        hop_copy(rc).wait_send()
        dir_copy(rc).wait_send()
        last_copy(rc).wait_send()


def shards(queries, keys, values, out_grad, members, centroids, proj_weight):
    vmem = pl.BlockSpec(memory_space=pltpu.VMEM)
    dma = pltpu.SemaphoreType.DMA
    return pl.pallas_call(
        kernel,
        out_shape=(
            jax.ShapeDtypeStruct((TOK, HEADS * HD), BF16),
            jax.ShapeDtypeStruct((HEADS, 1, HD), F32),
        ),
        in_specs=[vmem] * 7,
        out_specs=(vmem, vmem),
        scratch_shapes=[
            pltpu.VMEM((HEADS, TOK, 4 * HD), BF16),
            pltpu.VMEM((N, HEADS, TOK // 128, 128), F32),
            pltpu.VMEM((N, HEADS, TOK // 128, 128), F32),
            pltpu.VMEM((HEADS, 1, SLOTS), F32),
            pltpu.VMEM((HEADS, SLOTS, 128), F32),
            pltpu.VMEM((HEADS, TOK, 128), F32),
            pltpu.VMEM((BLK, SLOTS), BF16),
            pltpu.VMEM((HEADS, N, CAP, 4 * HD), BF16),
            pltpu.VMEM((HEADS, N, CAP, 4 * HD), BF16),
            pltpu.VMEM((W, 4 * HD), BF16),
            pltpu.VMEM((W, 3 * HD), BF16),
            pltpu.VMEM((W, HD), F32),
            pltpu.VMEM((W, HD), F32),
            pltpu.VMEM((W // BLK, BLK, BLK), F32),
            pltpu.VMEM((W // BLK, BLK, BLK), F32),
            pltpu.VMEM((HD, W), BF16),
            pltpu.VMEM((HEADS, N, CAP, 3 * HD), BF16),
            pltpu.VMEM((HEADS, N, CAP, 3 * HD), BF16),
            pltpu.VMEM((TOK, 3 * HEADS * HD), BF16),
            pltpu.VMEM((RC, 2, NY, RROWS, 256), BF16),
            pltpu.VMEM((RC, NY, RROWS, 256), BF16),
            pltpu.VMEM((RC, NY, RROWS, 256), BF16),
            pltpu.VMEM((RC, RROWS, 256), BF16),
            pltpu.VMEM((RC, RROWS, 256), BF16),
            pltpu.VMEM((RC, RROWS, 256), BF16),
            pltpu.VMEM((RC, RROWS, 256), BF16),
            dma((N,)), dma((N,)),
            dma((HEADS, N)), dma((HEADS, N)),
            dma((HEADS, N)), dma((HEADS, N)),
            dma((2, HEADS)),
            dma((RC,)), dma((RC,)),
            dma((RC,)), dma((RC,)),
            dma((RC,)), dma((RC,)),
            dma((RC,)), dma((RC,)),
        ],
        compiler_params=pltpu.CompilerParams(
            collective_id=0, has_side_effects=True, vmem_limit_bytes=60 * 1024 * 1024
        ),
    )(queries, keys, values, out_grad, members, centroids, proj_weight)


def solution(mesh):
    return jax.shard_map(
        shards,
        mesh=mesh,
        in_specs=(
            P("seq", "head"),
            P("seq", "head"),
            P("seq", "head"),
            P("seq", "head"),
            P("head", "seq", None),
            P("head", "seq", None),
            P(None, None, "head"),
        ),
        out_specs=(P("seq", "head"), P("head", "seq", None)),
        check_vma=False,
    )
```

```python
import math

import jax
import jax.numpy as jnp
from jax import lax
from jax.experimental import pallas as pl
from jax.experimental.pallas import tpu as pltpu
from jax.sharding import PartitionSpec as P

MESH = pl.DeviceIdType.MESH
F32 = jnp.float32
BF16 = jnp.bfloat16

decay_rate = 0.99

N = 32
NZ, NX = 8, 4
NY = 4
TOK = 1024
W = 1024
CAP = 64
HD = 128
HEADS = 2
SLOTS = N * CAP
GROUP = 4
BLK = 256
RC = 8
RROWS = TOK // RC
TILES = TOK // 128
SELF_STEP = (NZ - 1) * NX


def one_hot(mask):
    return jnp.where(mask, 1.0, 0.0).astype(BF16)


def iota(shape, dim):
    return lax.broadcasted_iota(jnp.int32, shape, dim).astype(F32)


def dot_nt(a, b):
    return lax.dot_general(a, b, (((1,), (1,)), ((), ())), preferred_element_type=F32)


def dot_nn(a, b):
    return jnp.dot(a, b, preferred_element_type=F32)


def kernel(
    q_hbm, k_hbm, v_hbm, g_hbm, mem_hbm, cent_hbm, w_hbm,
    out_ref, newc_ref,
    mem_ref, cent_ref, w_ref, in_sem, codes_w, tab, codes_s, codes_r, destrow, dest_t, slot_t, hot,
    stage_f, recv_f, x_ref, y_ref, dk_ref, dv_ref, p_scr, d_scr, k_t,
    stage_r, recv_r, first, part, part_r, p2, hop_r, hop_s, dir_r, last_r,
    code_ss, code_rs, fwd_ss, fwd_rs, ret_ss, ret_rs, self_sem,
    core_ss, core_rs, hop_ss, hop_rs, dir_ss, dir_rs, last_ss, last_rs,
):
    me = lax.axis_index("seq")
    hd = lax.axis_index("head")
    my_z, my_x = lax.div(me, NX), lax.rem(me, NX)
    my_y, core = lax.div(hd, 2), lax.rem(hd, 2)
    sibling = my_y * 2 + (1 - core)
    y_next = lax.rem(my_y + 1, NY)
    y_prev = lax.rem(my_y + NY - 1, NY)
    y_far = lax.rem(my_y + 2, NY)
    next_hd = y_next * 2 + core
    prev_hd = y_prev * 2 + core

    def peer(n):
        step = lax.div(n, NX)
        dx = lax.rem(n, NX)
        half = lax.div(step, 2)
        odd = lax.rem(step, 2)
        dz = jnp.where(step == NZ - 1, 0, jnp.where(odd == 1, NZ - 1 - half, 1 + half))
        return lax.rem(my_z + dz, NZ) * NX + lax.rem(my_x + dx, NX)

    barrier = pltpu.get_barrier_semaphore()

    def greet(n, carry):
        @pl.when(n != SELF_STEP)
        def _():
            pl.semaphore_signal(barrier, inc=1, device_id=(peer(n), hd), device_id_type=MESH)
        return carry

    lax.fori_loop(0, N, greet, 0)
    for other in (sibling, next_hd, prev_hd):
        pl.semaphore_signal(barrier, inc=1, device_id=(me, other), device_id_type=MESH)

    mem_in = pltpu.make_async_copy(mem_hbm, mem_ref, in_sem.at[0])
    mem_in.start()
    cent_in = pltpu.make_async_copy(cent_hbm, cent_ref, in_sem.at[1])
    cent_in.start()
    for h in range(HEADS):
        for at, ref in enumerate((q_hbm, k_hbm, v_hbm, g_hbm)):
            pltpu.make_async_copy(
                ref.at[:, h * HD : (h + 1) * HD], tab.at[h, :, at * HD : (at + 1) * HD], in_sem.at[2]
            ).start()
    for h in range(HEADS):
        for a in range(3):
            pltpu.make_async_copy(
                w_hbm.at[a, :, h * HD : (h + 1) * HD], w_ref.at[h, :, a * HD : (a + 1) * HD], in_sem.at[3]
            ).start()
    mem_in.wait()

    runs = []
    for h in range(HEADS):
        m = mem_ref[h]
        dev = lax.broadcasted_iota(jnp.int32, (N, W), 0)
        eq = (m >> 10) == dev
        start = jnp.sum(jnp.where((m >> 10) < dev, 1.0, 0.0), axis=1, keepdims=True)
        count = jnp.sum(jnp.where(eq, 1.0, 0.0), axis=1, keepdims=True)
        start_of = jnp.sum(jnp.where(eq, start, 0.0), axis=0, keepdims=True)
        rank = iota((1, W), 1) + 1.0 - start_of
        runs.append((start, count))
        ranks = jnp.where(
            (m >> 7) == lax.broadcasted_iota(jnp.int32, (N * TILES, W), 0), rank, 0.0
        ).astype(BF16)
        low = one_hot((m & 127) == lax.broadcasted_iota(jnp.int32, (128, W), 0))
        codes_w[:, h] = dot_nt(ranks, low).reshape(N, TILES, 128)
    codes_s[...] = codes_w[...].reshape(N, HEADS * TILES, 128).astype(BF16)

    pl.semaphore_wait(barrier, N - 1 + 3)

    def code_copy(src, dst, step, other):
        return pltpu.make_async_remote_copy(
            src_ref=src, dst_ref=dst, send_sem=code_ss.at[0], recv_sem=code_rs.at[step],
            device_id=(other, hd), device_id_type=MESH,
        )

    def send_codes(n, carry):
        @pl.when(n != SELF_STEP)
        def _():
            to = peer(n)
            step = lax.div(n, NX)
            swap = step + 1 - 2 * lax.rem(step, 2)
            there = jnp.where(step < NZ - 2, swap, step)
            code_copy(codes_s.at[to], codes_r.at[me], there, to).start()
        return carry

    def wait_codes(step, count):
        some = pl.ds(0, count)
        code_copy(codes_s.at[some], codes_r.at[some], step, me).wait_recv()

    lax.fori_loop(0, N, send_codes, 0)
    codes_r[me] = codes_s[me]

    for h in range(HEADS):
        start, count = runs[h]
        slot = lax.broadcasted_iota(jnp.int32, (N, SLOTS), 1)
        dev2 = lax.broadcasted_iota(jnp.int32, (N, SLOTS), 0)
        rank_at = (slot & (CAP - 1)).astype(F32)
        place = jnp.where(rank_at < count, start + rank_at, -1.0)
        destrow[h] = jnp.sum(jnp.where((slot >> 6) == dev2, place, 0.0), axis=0, keepdims=True)
    pltpu.make_async_copy(tab, tab, in_sem.at[2]).wait()

    def fwd_copy(h, src, dst, other):
        return pltpu.make_async_remote_copy(
            src_ref=stage_f.at[h, src], dst_ref=recv_f.at[h, dst],
            send_sem=fwd_ss.at[h], recv_sem=fwd_rs.at[h],
            device_id=(other, hd), device_id_type=MESH,
        )

    def ret_copy(h, src, dst, other):
        return pltpu.make_async_remote_copy(
            src_ref=stage_r.at[h, src], dst_ref=recv_r.at[h, dst],
            send_sem=ret_ss.at[h], recv_sem=ret_rs.at[h],
            device_id=(other, hd), device_id_type=MESH,
        )

    def fwd_self(h):
        return pltpu.make_async_copy(stage_f.at[h, SELF_STEP], recv_f.at[h, me], self_sem.at[0, h])

    def ret_self(h):
        return pltpu.make_async_copy(stage_r.at[h, SELF_STEP], recv_r.at[h, me], self_sem.at[1, h])

    def launch(h, gi, copy_of, self_of):
        for u in range(GROUP):
            n = gi * GROUP + u
            to = peer(n)

            @pl.when(n != SELF_STEP)
            def _():
                copy_of(h, n, me, to).start()

            @pl.when(n == SELF_STEP)
            def _():
                self_of(h).start()

    others = pl.ds(0, N - 1)

    def wait_all(h, copy_of, self_of):
        copy_of(h, others, others, me).wait_recv()
        self_of(h).wait()

    rank_rows = iota((CAP, 128), 0) + 1.0
    lanes = iota((CAP, 128), 1)

    def gather_head(h, carry):
        def group(gi, inner):
            @pl.when((h == 0) & (gi < NZ - 1))
            def _():
                wait_codes(gi, NX)

            @pl.when((h == 0) & (gi == NZ - 1))
            def _():
                wait_codes(gi, NX - 1)

            for u in range(GROUP):
                to = peer(gi * GROUP + u)

                @pl.when(h == 0)
                def _():
                    codes_w[to] = codes_r[to].astype(F32).reshape(HEADS, TILES, 128)

                for tc in range(TILES):
                    row = codes_w[to, h, tc : tc + 1, :]
                    hot[u * CAP : (u + 1) * CAP, tc * 128 : (tc + 1) * 128] = one_hot(row == rank_rows)
            rows = dot_nn(hot[:, :TOK], tab[h])
            stage_f[h, pl.ds(gi * GROUP, GROUP)] = rows.astype(BF16).reshape(GROUP, CAP, 4 * HD)
            launch(h, gi, fwd_copy, fwd_self)
            return inner

        return lax.fori_loop(0, N // GROUP, group, carry)

    lax.fori_loop(0, HEADS, gather_head, 0)

    for h in range(HEADS):
        dest_t[h] = jnp.transpose(jnp.broadcast_to(destrow[h], (128, SLOTS)))
    for h in range(HEADS):
        slot = jnp.zeros((TILES, 128), F32)
        for c in range(N):
            code = codes_w[c, h]
            slot = slot + jnp.where(code > 0.0, code + (c * CAP - 1.0), 0.0)
        for tc in range(TILES):
            slot_t[h, tc * 128 : (tc + 1) * 128, :] = jnp.transpose(
                jnp.broadcast_to(slot[tc : tc + 1, :], (128, 128))
            )

    exp_scale = math.log2(math.e) / math.sqrt(HD)
    scale = 1.0 / math.sqrt(HD)
    causal = lax.broadcasted_iota(jnp.int32, (BLK, BLK), 0) <= lax.broadcasted_iota(
        jnp.int32, (BLK, BLK), 1
    )

    cent_in.wait()

    def cluster_head(h, carry):
        wait_all(h, fwd_copy, fwd_self)

        def order(ib, sums):
            place = iota((BLK, 128), 0) + (ib * BLK).astype(F32)
            for pc in range(SLOTS // 128):
                row = destrow[h, :, pc * 128 : (pc + 1) * 128]
                hot[:, pc * 128 : (pc + 1) * 128] = one_hot(row == place)
            rows = dot_nn(hot[...], recv_f[h].reshape(SLOTS, 4 * HD))
            x_ref[pl.ds(ib * BLK, BLK), :] = rows.astype(BF16)
            return sums + jnp.sum(rows[:, :HD] + rows[:, HD : 2 * HD], axis=0, keepdims=True)

        sums = lax.fori_loop(0, W // BLK, order, jnp.zeros((1, HD), F32))
        newc_ref[h] = decay_rate * cent_ref[h] + 0.5 * (1.0 - decay_rate) * sums

        k_t[...] = jnp.transpose(x_ref[:, HD : 2 * HD].astype(F32)).astype(BF16)

        for b in range(W // BLK):
            low = b * BLK
            q_b = x_ref[low : low + BLK, 0:HD]
            g_b = x_ref[low : low + BLK, 3 * HD : 4 * HD]
            top = None
            for jb in range(b + 1):
                s = dot_nt(x_ref[jb * BLK : (jb + 1) * BLK, HD : 2 * HD], q_b)
                if jb == b:
                    s = jnp.where(causal, s, -jnp.inf)
                p_scr[jb] = s
                part_top = jnp.max(s, axis=0, keepdims=True)
                top = part_top if top is None else jnp.maximum(top, part_top)
            total = jnp.zeros((1, BLK), F32)
            delta = jnp.zeros((1, BLK), F32)
            for jb in range(b + 1):
                p = jnp.exp2((p_scr[jb] - top) * exp_scale)
                d = dot_nt(x_ref[jb * BLK : (jb + 1) * BLK, 2 * HD : 3 * HD], g_b)
                p_scr[jb] = p
                d_scr[jb] = d
                total = total + jnp.sum(p, axis=0, keepdims=True)
                delta = delta + jnp.sum(p * d, axis=0, keepdims=True)
            inv = 1.0 / total
            delta = delta * inv
            dq_t = jnp.zeros((HD, BLK), F32)
            for jb in range(b + 1):
                rows = slice(jb * BLK, (jb + 1) * BLK)
                p = p_scr[jb] * inv
                p_low = p.astype(BF16)
                ds = (p * (d_scr[jb] - delta)).astype(BF16)
                dv = dot_nn(p_low, g_b)
                dk = dot_nn(ds, q_b)
                dq_t = dq_t + dot_nn(k_t[:, rows], ds)
                if jb == b:
                    dv_ref[rows, :] = dv
                    dk_ref[rows, :] = dk
                else:
                    dv_ref[rows, :] += dv
                    dk_ref[rows, :] += dk
            y_ref[low : low + BLK, 0:HD] = (jnp.transpose(dq_t) * scale).astype(BF16)
        y_ref[:, HD : 2 * HD] = (dk_ref[...] * scale).astype(BF16)
        y_ref[:, 2 * HD : 3 * HD] = dv_ref[...].astype(BF16)

        def group(gi, inner):
            for u in range(GROUP):
                to = peer(gi * GROUP + u)
                place = dest_t[h, pl.ds(pl.multiple_of(to * CAP, CAP), CAP), :]
                for ic in range(W // 128):
                    hot[u * CAP : (u + 1) * CAP, ic * 128 : (ic + 1) * 128] = one_hot(
                        place == lanes + ic * 128.0
                    )
            rows = dot_nn(hot[:, :W], y_ref[...])
            stage_r[h, pl.ds(gi * GROUP, GROUP)] = rows.astype(BF16).reshape(GROUP, CAP, 3 * HD)
            launch(h, gi, ret_copy, ret_self)
            return inner

        return lax.fori_loop(0, N // GROUP, group, carry)

    lax.fori_loop(0, HEADS, cluster_head, 0)

    for h in range(HEADS):
        fwd_copy(h, others, others, me).wait_send()
    pltpu.make_async_copy(w_ref, w_ref, in_sem.at[3]).wait()

    wide = iota((BLK, 128), 1)

    def put_hot(h, tb, carry):
        rows_at = pl.ds(pl.multiple_of(tb * BLK, BLK), BLK)
        place = slot_t[h, rows_at, :]
        for pc in range(SLOTS // 128):
            part_at, lane = divmod(pc * 128, 4 * HD)
            block = one_hot(place == wide + pc * 128.0).reshape(BLK // CAP, CAP, 128)
            some = pl.ds(part_at % 2 * (TOK // CAP) + tb * (BLK // CAP), BLK // CAP)
            stage_f[part_at // 2, some, :, lane : lane + 128] = block
        return carry

    def tokens(h, tb):
        acc = None
        for part_at in range(SLOTS // (4 * HD)):
            some = pl.ds(part_at % 2 * (TOK // CAP) + tb * (BLK // CAP), BLK // CAP)
            hots = stage_f[part_at // 2, some].reshape(BLK, 4 * HD)
            runs_at = 4 * HD // CAP
            rows = recv_r[h, part_at * runs_at : (part_at + 1) * runs_at].reshape(4 * HD, 3 * HD)
            term = dot_nn(hots, rows)
            acc = term if acc is None else acc + term
        return acc.astype(BF16)

    lax.fori_loop(0, TOK // BLK, lambda tb, c: put_hot(0, tb, c), 0)
    wait_all(0, ret_copy, ret_self)

    def first_part(tb, carry):
        z = tokens(0, tb)
        rows_at = pl.ds(pl.multiple_of(tb * BLK, BLK), BLK)

        def one(d, inner):
            w_d = w_ref[0, pl.ds(pl.multiple_of(d * 256, 256), 256), :]
            first[d, rows_at, :] = dot_nt(z, w_d)
            return inner

        return lax.fori_loop(0, 2 * NY, one, carry)

    lax.fori_loop(0, TOK // BLK, first_part, 0)
    lax.fori_loop(0, TOK // BLK, lambda tb, c: put_hot(1, tb, c), 0)
    wait_all(1, ret_copy, ret_self)

    def y_copy(src, dst, send_sem, recv_sem, other):
        return pltpu.make_async_remote_copy(
            src_ref=src, dst_ref=dst, send_sem=send_sem, recv_sem=recv_sem,
            device_id=(me, other), device_id_type=MESH,
        )

    def onward(rc):
        return (next_hd, y_next) if rc % 2 == 0 else (prev_hd, y_prev)

    def back(rc):
        return (prev_hd, y_prev) if rc % 2 == 0 else (next_hd, y_next)

    def core_copy(rc):
        return y_copy(part.at[rc, 1 - core], part_r.at[rc], core_ss.at[0], core_rs.at[rc], sibling)

    def hop_copy(rc):
        return y_copy(p2.at[rc, y_far], hop_r.at[rc], hop_ss.at[0], hop_rs.at[rc], onward(rc)[0])

    def dir_copy(rc):
        other, its_y = back(rc)
        return y_copy(p2.at[rc, its_y], dir_r.at[rc], dir_ss.at[0], dir_rs.at[rc], other)

    def last_copy(rc):
        return y_copy(hop_s.at[rc], last_r.at[rc], last_ss.at[0], last_rs.at[rc], onward(rc)[0])

    per = BLK // RROWS

    def project(tb):
        z = tokens(1, tb)

        def half(side):
            def one(yy, carry):
                d = yy * 2 + side
                w_d = w_ref[1, pl.ds(pl.multiple_of(d * 256, 256), 256), :]
                low = (first[d, tb * BLK : (tb + 1) * BLK, :] + dot_nt(z, w_d)).astype(BF16)
                for piece in range(per):
                    part[tb * per + piece, side, yy] = low[piece * RROWS : (piece + 1) * RROWS]
                return carry

            lax.fori_loop(0, NY, one, 0)

        half(1 - core)
        for piece in range(per):
            core_copy(tb * per + piece).start()
        half(core)

    def merge(rc):
        core_copy(rc).wait_recv()
        p2[rc] = (part[rc, core].astype(F32) + part_r[rc].astype(F32)).astype(BF16)
        hop_copy(rc).start()
        dir_copy(rc).start()

    def relay(rc):
        hop_copy(rc).wait_recv()
        mine = p2[rc, onward(rc)[1]]
        hop_s[rc] = (hop_r[rc].astype(F32) + mine.astype(F32)).astype(BF16)
        last_copy(rc).start()

    def finish(rc):
        dir_copy(rc).wait_recv()
        last_copy(rc).wait_recv()
        total = p2[rc, my_y].astype(F32) + dir_r[rc].astype(F32) + last_r[rc].astype(F32)
        out_ref[rc * RROWS : (rc + 1) * RROWS, :] = total.astype(BF16)

    for step in range(TOK // BLK + 3):
        if step < TOK // BLK:
            project(step)
        if 1 <= step <= TOK // BLK:
            for rc in range((step - 1) * per, step * per):
                merge(rc)
        if 2 <= step <= TOK // BLK + 1:
            for rc in range((step - 2) * per, (step - 1) * per):
                relay(rc)
    for rc in range(RC):
        finish(rc)

    code_copy(codes_s.at[others], codes_r.at[others], 0, me).wait_send()
    for h in range(HEADS):
        ret_copy(h, others, others, me).wait_send()
    chunks = pl.ds(0, RC)
    y_copy(part.at[chunks, 0], part_r, core_ss.at[0], core_rs.at[0], sibling).wait_send()
    for sem in (hop_ss, dir_ss, last_ss):
        y_copy(p2.at[chunks, 0], p2.at[chunks, 0], sem.at[0], hop_rs.at[0], next_hd).wait_send()


def shards(queries, keys, values, out_grad, members, centroids, proj_weight):
    vmem = pl.BlockSpec(memory_space=pltpu.VMEM)
    dma = pltpu.SemaphoreType.DMA
    return pl.pallas_call(
        kernel,
        out_shape=(
            jax.ShapeDtypeStruct((TOK, HEADS * HD), BF16),
            jax.ShapeDtypeStruct((HEADS, 1, HD), F32),
        ),
        in_specs=[pl.BlockSpec(memory_space=pl.ANY)] * 7,
        out_specs=(vmem, vmem),
        scratch_shapes=[
            pltpu.VMEM((HEADS, 1, W), jnp.int32),
            pltpu.VMEM((HEADS, 1, HD), F32),
            pltpu.VMEM((HEADS, 2048, 3 * HD), BF16),
            dma((4,)),
            pltpu.VMEM((N, HEADS, TILES, 128), F32),
            pltpu.VMEM((HEADS, TOK, 4 * HD), BF16),
            pltpu.VMEM((N, HEADS * TILES, 128), BF16),
            pltpu.VMEM((N, HEADS * TILES, 128), BF16),
            pltpu.VMEM((HEADS, 1, SLOTS), F32),
            pltpu.VMEM((HEADS, SLOTS, 128), F32),
            pltpu.VMEM((HEADS, TOK, 128), F32),
            pltpu.VMEM((BLK, SLOTS), BF16),
            pltpu.VMEM((HEADS, N, CAP, 4 * HD), BF16),
            pltpu.VMEM((HEADS, N, CAP, 4 * HD), BF16),
            pltpu.VMEM((W, 4 * HD), BF16),
            pltpu.VMEM((W, 3 * HD), BF16),
            pltpu.VMEM((W, HD), F32),
            pltpu.VMEM((W, HD), F32),
            pltpu.VMEM((W // BLK, BLK, BLK), F32),
            pltpu.VMEM((W // BLK, BLK, BLK), F32),
            pltpu.VMEM((HD, W), BF16),
            pltpu.VMEM((HEADS, N, CAP, 3 * HD), BF16),
            pltpu.VMEM((HEADS, N, CAP, 3 * HD), BF16),
            pltpu.VMEM((2 * NY, TOK, 256), F32),
            pltpu.VMEM((RC, 2, NY, RROWS, 256), BF16),
            pltpu.VMEM((RC, NY, RROWS, 256), BF16),
            pltpu.VMEM((RC, NY, RROWS, 256), BF16),
            pltpu.VMEM((RC, RROWS, 256), BF16),
            pltpu.VMEM((RC, RROWS, 256), BF16),
            pltpu.VMEM((RC, RROWS, 256), BF16),
            pltpu.VMEM((RC, RROWS, 256), BF16),
            dma((1,)), dma((NZ,)),
            dma((HEADS,)), dma((HEADS,)),
            dma((HEADS,)), dma((HEADS,)),
            dma((2, HEADS)),
            dma((1,)), dma((RC,)),
            dma((1,)), dma((RC,)),
            dma((1,)), dma((RC,)),
            dma((1,)), dma((RC,)),
        ],
        compiler_params=pltpu.CompilerParams(
            collective_id=0, has_side_effects=True, vmem_limit_bytes=60 * 1024 * 1024
        ),
    )(queries, keys, values, out_grad, members, centroids, proj_weight)


def solution(mesh):
    return jax.shard_map(
        shards,
        mesh=mesh,
        in_specs=(
            P("seq", "head"),
            P("seq", "head"),
            P("seq", "head"),
            P("seq", "head"),
            P("head", "seq", None),
            P("head", "seq", None),
            P(None, None, "head"),
        ),
        out_specs=(P("seq", "head"), P("head", "seq", None)),
        check_vma=False,
    )
```

```python
import math

import jax
import jax.numpy as jnp
from jax import lax
from jax.experimental import pallas as pl
from jax.experimental.pallas import tpu as pltpu
from jax.sharding import PartitionSpec as P

MESH = pl.DeviceIdType.MESH
F32 = jnp.float32
BF16 = jnp.bfloat16

decay_rate = 0.99

N = 32
NZ, NX = 8, 4
NY = 4
TOK = 1024
W = 1024
CAP = 64
HD = 128
HEADS = 2
SLOTS = N * CAP
GROUP = 4
BLK = 256
HALF = TOK // 2
TILES = TOK // 128
LEVELS = NZ // 2
SELF_STEP = 1


def one_hot(mask):
    return jnp.where(mask, 1.0, 0.0).astype(BF16)


def iota(shape, dim):
    return lax.broadcasted_iota(jnp.int32, shape, dim).astype(F32)


def dot_nt(a, b):
    return lax.dot_general(a, b, (((1,), (1,)), ((), ())), preferred_element_type=F32)


def dot_nn(a, b):
    return jnp.dot(a, b, preferred_element_type=F32)


def kernel(
    q_hbm, k_hbm, v_hbm, g_hbm, mem_hbm, cent_hbm, w_hbm,
    out_ref, newc_ref,
    mem_ref, cent_ref, w_ref, in_sem, codes_w, tab, codes_s, codes_r, destrow, dest_t, slot_t, hot,
    stage_f, recv_f, x_ref, y_ref, dk_ref, dv_ref, p_scr, d_scr, k_t,
    stage_r, recv_r, first, z_sum, z_ref, own, part, part_r, p2, hop_r, hop_s, dir_r, last_r,
    code_ss, code_rs, fwd_ss, fwd_rs, ret_ss, ret_rs, self_sem,
    core_ss, core_rs, hop_ss, hop_rs, dir_ss, dir_rs, last_ss, last_rs,
):
    me = lax.axis_index("seq")
    hd = lax.axis_index("head")
    my_z, my_x = lax.div(me, NX), lax.rem(me, NX)
    my_y, core = lax.div(hd, 2), lax.rem(hd, 2)
    sibling = my_y * 2 + (1 - core)
    y_next = lax.rem(my_y + 1, NY)
    y_prev = lax.rem(my_y + NY - 1, NY)
    y_far = lax.rem(my_y + 2, NY)
    next_hd = y_next * 2 + core
    prev_hd = y_prev * 2 + core

    def level_z(level, side):
        dz = jnp.where(side == 0, NZ // 2 - level, jnp.where(level == 0, 0, NZ // 2 + level))
        return lax.rem(my_z + dz, NZ)

    def peer(n):
        in_level = lax.rem(n, 2 * NX)
        dx = lax.div(in_level, 2)
        return level_z(lax.div(n, 2 * NX), lax.rem(in_level, 2)) * NX + lax.rem(my_x + dx, NX)

    barrier = pltpu.get_barrier_semaphore()

    def greet(n, carry):
        @pl.when(n != SELF_STEP)
        def _():
            pl.semaphore_signal(barrier, inc=1, device_id=(peer(n), hd), device_id_type=MESH)
        return carry

    lax.fori_loop(0, N, greet, 0)
    for other in (sibling, next_hd, prev_hd):
        pl.semaphore_signal(barrier, inc=1, device_id=(me, other), device_id_type=MESH)

    mem_in = pltpu.make_async_copy(mem_hbm, mem_ref, in_sem.at[0])
    mem_in.start()
    cent_in = pltpu.make_async_copy(cent_hbm, cent_ref, in_sem.at[1])
    cent_in.start()
    for h in range(HEADS):
        for at, ref in enumerate((q_hbm, k_hbm, v_hbm, g_hbm)):
            pltpu.make_async_copy(
                ref.at[:, h * HD : (h + 1) * HD], tab.at[h, :, at * HD : (at + 1) * HD], in_sem.at[2]
            ).start()
    for h in range(HEADS):
        for a in range(3):
            pltpu.make_async_copy(
                w_hbm.at[a, :, h * HD : (h + 1) * HD], w_ref.at[h, :, a * HD : (a + 1) * HD], in_sem.at[3]
            ).start()
    mem_in.wait()

    runs = []
    for h in range(HEADS):
        m = mem_ref[h]
        dev = lax.broadcasted_iota(jnp.int32, (N, W), 0)
        eq = (m >> 10) == dev
        start = jnp.sum(jnp.where((m >> 10) < dev, 1.0, 0.0), axis=1, keepdims=True)
        count = jnp.sum(jnp.where(eq, 1.0, 0.0), axis=1, keepdims=True)
        start_of = jnp.sum(jnp.where(eq, start, 0.0), axis=0, keepdims=True)
        rank = iota((1, W), 1) + 1.0 - start_of
        runs.append((start, count))
        ranks = jnp.where(
            (m >> 7) == lax.broadcasted_iota(jnp.int32, (N * TILES, W), 0), rank, 0.0
        ).astype(BF16)
        low = one_hot((m & 127) == lax.broadcasted_iota(jnp.int32, (128, W), 0))
        codes_w[:, h] = dot_nt(ranks, low).reshape(N, TILES, 128)
    codes_s[...] = codes_w[...].reshape(N, HEADS * TILES, 128).astype(BF16)

    pl.semaphore_wait(barrier, N - 1 + 3)

    def code_copy(src, dst, step, other):
        return pltpu.make_async_remote_copy(
            src_ref=src, dst_ref=dst, send_sem=code_ss.at[0], recv_sem=code_rs.at[step],
            device_id=(other, hd), device_id_type=MESH,
        )

    def send_codes(n, carry):
        @pl.when(n != SELF_STEP)
        def _():
            to = peer(n)
            code_copy(codes_s.at[to], codes_r.at[me], lax.div(n, 2 * NX), to).start()
        return carry

    def wait_codes(step, count):
        some = pl.ds(0, count)
        code_copy(codes_s.at[some], codes_r.at[some], step, me).wait_recv()

    lax.fori_loop(0, N, send_codes, 0)
    codes_r[me] = codes_s[me]

    for h in range(HEADS):
        start, count = runs[h]
        slot = lax.broadcasted_iota(jnp.int32, (N, SLOTS), 1)
        dev2 = lax.broadcasted_iota(jnp.int32, (N, SLOTS), 0)
        rank_at = (slot & (CAP - 1)).astype(F32)
        place = jnp.where(rank_at < count, start + rank_at, -1.0)
        destrow[h] = jnp.sum(jnp.where((slot >> 6) == dev2, place, 0.0), axis=0, keepdims=True)
    pltpu.make_async_copy(tab, tab, in_sem.at[2]).wait()

    def fwd_copy(h, src, dst, other):
        return pltpu.make_async_remote_copy(
            src_ref=stage_f.at[h, src], dst_ref=recv_f.at[h, dst],
            send_sem=fwd_ss.at[h], recv_sem=fwd_rs.at[h],
            device_id=(other, hd), device_id_type=MESH,
        )

    def ret_copy(h, src, dst, other, step):
        return pltpu.make_async_remote_copy(
            src_ref=stage_r.at[h, src], dst_ref=recv_r.at[h, dst],
            send_sem=ret_ss.at[h], recv_sem=ret_rs.at[h, step],
            device_id=(other, hd), device_id_type=MESH,
        )

    def fwd_self(h):
        return pltpu.make_async_copy(stage_f.at[h, SELF_STEP], recv_f.at[h, me], self_sem.at[0, h])

    def ret_self(h):
        return pltpu.make_async_copy(stage_r.at[h, SELF_STEP], recv_r.at[h, me], self_sem.at[1, h])

    def launch(gi, copy_of, self_copy):
        for u in range(GROUP):
            n = gi * GROUP + u
            to = peer(n)

            @pl.when(n != SELF_STEP)
            def _():
                copy_of(n, to).start()

            @pl.when(n == SELF_STEP)
            def _():
                self_copy.start()

    others = pl.ds(0, N - 1)

    def wait_ret(h, step):
        some = pl.ds(0, 2 * NX - (step == 0))
        ret_copy(h, some, some, me, step).wait_recv()
        if step == 0:
            ret_self(h).wait()

    rank_rows = iota((CAP, 128), 0) + 1.0
    lanes = iota((CAP, 128), 1)

    def gather_head(h, carry):
        def group(gi, inner):
            @pl.when((h == 0) & (gi == 0))
            def _():
                wait_codes(0, 2 * NX - 1)

            @pl.when((h == 0) & (gi > 0) & (lax.rem(gi, 2) == 0))
            def _():
                wait_codes(lax.div(gi, 2), 2 * NX)

            for u in range(GROUP):
                to = peer(gi * GROUP + u)

                @pl.when(h == 0)
                def _():
                    codes_w[to] = codes_r[to].astype(F32).reshape(HEADS, TILES, 128)

                for tc in range(TILES):
                    row = codes_w[to, h, tc : tc + 1, :]
                    hot[u * CAP : (u + 1) * CAP, tc * 128 : (tc + 1) * 128] = one_hot(row == rank_rows)
            rows = dot_nn(hot[:, :TOK], tab[h])
            stage_f[h, pl.ds(gi * GROUP, GROUP)] = rows.astype(BF16).reshape(GROUP, CAP, 4 * HD)
            launch(gi, lambda n, to: fwd_copy(h, n, me, to), fwd_self(h))
            return inner

        return lax.fori_loop(0, N // GROUP, group, carry)

    lax.fori_loop(0, HEADS, gather_head, 0)

    for h in range(HEADS):
        dest_t[h] = jnp.transpose(jnp.broadcast_to(destrow[h], (128, SLOTS)))
    for h in range(HEADS):
        slot = jnp.zeros((TILES, 128), F32)
        for c in range(N):
            code = codes_w[c, h]
            slot = slot + jnp.where(code > 0.0, code + (c * CAP - 1.0), 0.0)
        for tc in range(TILES):
            slot_t[h, tc * 128 : (tc + 1) * 128, :] = jnp.transpose(
                jnp.broadcast_to(slot[tc : tc + 1, :], (128, 128))
            )

    exp_scale = math.log2(math.e) / math.sqrt(HD)
    scale = 1.0 / math.sqrt(HD)
    causal = lax.broadcasted_iota(jnp.int32, (BLK, BLK), 0) <= lax.broadcasted_iota(
        jnp.int32, (BLK, BLK), 1
    )

    cent_in.wait()

    def cluster_head(h, carry):
        fwd_copy(h, others, others, me).wait_recv()
        fwd_self(h).wait()

        def order(ib, sums):
            place = iota((BLK, 128), 0) + (ib * BLK).astype(F32)
            for pc in range(SLOTS // 128):
                row = destrow[h, :, pc * 128 : (pc + 1) * 128]
                hot[:, pc * 128 : (pc + 1) * 128] = one_hot(row == place)
            rows = dot_nn(hot[...], recv_f[h].reshape(SLOTS, 4 * HD))
            x_ref[pl.ds(ib * BLK, BLK), :] = rows.astype(BF16)
            return sums + jnp.sum(rows[:, :HD] + rows[:, HD : 2 * HD], axis=0, keepdims=True)

        sums = lax.fori_loop(0, W // BLK, order, jnp.zeros((1, HD), F32))
        newc_ref[h] = decay_rate * cent_ref[h] + 0.5 * (1.0 - decay_rate) * sums

        k_t[...] = jnp.transpose(x_ref[:, HD : 2 * HD].astype(F32)).astype(BF16)

        for b in range(W // BLK):
            low = b * BLK
            q_b = x_ref[low : low + BLK, 0:HD]
            g_b = x_ref[low : low + BLK, 3 * HD : 4 * HD]
            top = None
            for jb in range(b + 1):
                s = dot_nt(x_ref[jb * BLK : (jb + 1) * BLK, HD : 2 * HD], q_b)
                if jb == b:
                    s = jnp.where(causal, s, -jnp.inf)
                p_scr[jb] = s
                part_top = jnp.max(s, axis=0, keepdims=True)
                top = part_top if top is None else jnp.maximum(top, part_top)
            total = jnp.zeros((1, BLK), F32)
            delta = jnp.zeros((1, BLK), F32)
            for jb in range(b + 1):
                p = jnp.exp2((p_scr[jb] - top) * exp_scale)
                d = dot_nt(x_ref[jb * BLK : (jb + 1) * BLK, 2 * HD : 3 * HD], g_b)
                p_scr[jb] = p
                d_scr[jb] = d
                total = total + jnp.sum(p, axis=0, keepdims=True)
                delta = delta + jnp.sum(p * d, axis=0, keepdims=True)
            inv = 1.0 / total
            delta = delta * inv
            dq_t = jnp.zeros((HD, BLK), F32)
            for jb in range(b + 1):
                rows = slice(jb * BLK, (jb + 1) * BLK)
                p = p_scr[jb] * inv
                p_low = p.astype(BF16)
                ds = (p * (d_scr[jb] - delta)).astype(BF16)
                dv = dot_nn(p_low, g_b)
                dk = dot_nn(ds, q_b)
                dq_t = dq_t + dot_nn(k_t[:, rows], ds)
                if jb == b:
                    dv_ref[rows, :] = dv
                    dk_ref[rows, :] = dk
                else:
                    dv_ref[rows, :] += dv
                    dk_ref[rows, :] += dk
            y_ref[low : low + BLK, 0:HD] = (jnp.transpose(dq_t) * scale).astype(BF16)
        y_ref[:, HD : 2 * HD] = (dk_ref[...] * scale).astype(BF16)
        y_ref[:, 2 * HD : 3 * HD] = dv_ref[...].astype(BF16)

        def group(gi, inner):
            for u in range(GROUP):
                to = peer(gi * GROUP + u)
                place = dest_t[h, pl.ds(pl.multiple_of(to * CAP, CAP), CAP), :]
                for ic in range(W // 128):
                    hot[u * CAP : (u + 1) * CAP, ic * 128 : (ic + 1) * 128] = one_hot(
                        place == lanes + ic * 128.0
                    )
            rows = dot_nn(hot[:, :W], y_ref[...])
            stage_r[h, pl.ds(gi * GROUP, GROUP)] = rows.astype(BF16).reshape(GROUP, CAP, 3 * HD)
            launch(gi, lambda n, to: ret_copy(h, n, me, to, lax.div(gi, 2)), ret_self(h))
            return inner

        return lax.fori_loop(0, N // GROUP, group, carry)

    lax.fori_loop(0, HEADS, cluster_head, 0)

    for h in range(HEADS):
        fwd_copy(h, others, others, me).wait_send()
    pltpu.make_async_copy(w_ref, w_ref, in_sem.at[3]).wait()

    wide = iota((BLK, 128), 1)

    def put_hot(h, tb, carry):
        rows_at = pl.ds(pl.multiple_of(tb * BLK, BLK), BLK)
        place = slot_t[h, rows_at, :]
        for pc in range(SLOTS // 128):
            part_at, lane = divmod(pc * 128, 4 * HD)
            block = one_hot(place == wide + pc * 128.0).reshape(BLK // CAP, CAP, 128)
            some = pl.ds(part_at % 2 * (TOK // CAP) + tb * (BLK // CAP), BLK // CAP)
            stage_f[part_at // 2, some, :, lane : lane + 128] = block
        return carry

    def tokens(h, tb):
        acc = None
        for part_at in range(SLOTS // (4 * HD)):
            some = pl.ds(part_at % 2 * (TOK // CAP) + tb * (BLK // CAP), BLK // CAP)
            hots = stage_f[part_at // 2, some].reshape(BLK, 4 * HD)
            runs_at = 4 * HD // CAP
            rows = recv_r[h, part_at * runs_at : (part_at + 1) * runs_at].reshape(4 * HD, 3 * HD)
            term = dot_nn(hots, rows)
            acc = term if acc is None else acc + term
        return acc.astype(BF16)

    def tokens_step(step):
        for half in range(2):
            term = None
            for side in range(2):
                at_z = level_z(step, side)
                lane = pl.ds(pl.multiple_of(lax.rem(at_z, 2) * (NX * CAP), NX * CAP), NX * CAP)
                rows = recv_r[1, pl.ds(at_z * NX, NX)].reshape(NX * CAP, 3 * HD)
                low = lax.rem(lax.div(at_z, 2), 2) * (TOK // CAP) + half * (HALF // CAP)
                hots = stage_f[lax.div(at_z, 4), pl.ds(low, HALF // CAP), :, lane].reshape(HALF, NX * CAP)
                more = dot_nn(hots, rows)
                term = more if term is None else term + more
            at = slice(half * HALF, (half + 1) * HALF)
            if step == 0:
                z_sum[at, :] = term
            elif step < LEVELS - 1:
                z_sum[at, :] += term
            else:
                z_ref[at, :] = (z_sum[at, :] + term).astype(BF16)

    lax.fori_loop(0, TOK // BLK, lambda tb, c: put_hot(0, tb, c), 0)
    for step in range(LEVELS):
        wait_ret(0, step)

    def first_part(tb, carry):
        z = tokens(0, tb)
        rows_at = pl.ds(pl.multiple_of(tb * BLK, BLK), BLK)

        def one(d, inner):
            w_d = w_ref[0, pl.ds(pl.multiple_of(d * 256, 256), 256), :]
            first[d, rows_at, :] = dot_nt(z, w_d)
            return inner

        return lax.fori_loop(0, 2 * NY, one, carry)

    lax.fori_loop(0, TOK // BLK, first_part, 0)
    lax.fori_loop(0, TOK // BLK, lambda tb, c: put_hot(1, tb, c), 0)
    for step in range(LEVELS):
        wait_ret(1, step)
        tokens_step(step)

    def y_copy(src, dst, send_sem, recv_sem, other):
        return pltpu.make_async_remote_copy(
            src_ref=src, dst_ref=dst, send_sem=send_sem, recv_sem=recv_sem,
            device_id=(me, other), device_id_type=MESH,
        )

    blocks = (y_far, y_next, y_prev, my_y)
    halves = (slice(0, HALF), slice(HALF, TOK))

    def core_copy(r, f):
        return y_copy(
            part.at[r, halves[f]], part_r.at[r, halves[f]], core_ss.at[0], core_rs.at[r, f], sibling
        )

    def hop_copy(f):
        return y_copy(
            p2.at[0, halves[f]], hop_r.at[f], hop_ss.at[0], hop_rs.at[f], (next_hd, prev_hd)[f]
        )

    def dir_copy(f):
        return y_copy(
            p2.at[2 - f, halves[f]], dir_r.at[f], dir_ss.at[0], dir_rs.at[f], (prev_hd, next_hd)[f]
        )

    def last_copy(f):
        return y_copy(hop_s.at[f], last_r.at[f], last_ss.at[0], last_rs.at[f], (next_hd, prev_hd)[f])

    def block(r, side, half):
        d = blocks[r] * 2 + side
        w_d = w_ref[1, pl.ds(pl.multiple_of(d * 256, 256), 256), :]
        return first[d, half, :] + dot_nt(z_ref[half, :], w_d)

    def theirs(r):
        for f in range(2):
            part[r, halves[f], :] = block(r, 1 - core, halves[f]).astype(BF16)
            core_copy(r, f).start()

    def ours(r):
        for half in halves:
            own[half, :] = block(r, core, half)

    def merge(r, f):
        core_copy(r, f).wait_recv()
        half = halves[f]
        p2[r, half, :] = (own[half, :] + part_r[r, half, :].astype(F32)).astype(BF16)

    def relay(f):
        hop_copy(f).wait_recv()
        hop_s[f] = (hop_r[f].astype(F32) + p2[1 + f, halves[f], :].astype(F32)).astype(BF16)
        last_copy(f).start()

    theirs(0)
    ours(0)
    theirs(1)
    for f in range(2):
        merge(0, f)
        hop_copy(f).start()
    theirs(2)
    ours(1)
    merge(1, 1)
    dir_copy(1).start()
    merge(1, 0)
    ours(2)
    merge(2, 0)
    dir_copy(0).start()
    merge(2, 1)
    theirs(3)
    relay(0)
    relay(1)
    ours(3)
    for f in range(2):
        core_copy(3, f).wait_recv()
        own[halves[f], :] += part_r[3, halves[f], :].astype(F32)
    for f in range(2):
        dir_copy(f).wait_recv()
        own[halves[f], :] += dir_r[f].astype(F32)
    for f in range(2):
        last_copy(f).wait_recv()
        out_ref[halves[f], :] = (own[halves[f], :] + last_r[f].astype(F32)).astype(BF16)

    code_copy(codes_s.at[others], codes_r.at[others], 0, me).wait_send()
    for h in range(HEADS):
        ret_copy(h, others, others, me, 0).wait_send()
    y_copy(part, part_r, core_ss.at[0], core_rs.at[0, 0], sibling).wait_send()
    for sem in (hop_ss, dir_ss, last_ss):
        y_copy(hop_s, hop_r, sem.at[0], hop_rs.at[0], next_hd).wait_send()


def hand_over(grad_ref, cent_ref, out_ref, newc_ref):
    out_ref[...] = grad_ref[...]
    newc_ref[...] = cent_ref[...]


def shards(queries, keys, values, out_grad, members, centroids, proj_weight):
    vmem = pl.BlockSpec(memory_space=pltpu.VMEM)
    dma = pltpu.SemaphoreType.DMA
    results = pl.pallas_call(
        kernel,
        out_shape=(
            jax.ShapeDtypeStruct((TOK, HEADS * HD), BF16),
            jax.ShapeDtypeStruct((HEADS, 1, HD), F32),
        ),
        in_specs=[pl.BlockSpec(memory_space=pl.ANY)] * 7,
        out_specs=(vmem, vmem),
        scratch_shapes=[
            pltpu.VMEM((HEADS, 1, W), jnp.int32),
            pltpu.VMEM((HEADS, 1, HD), F32),
            pltpu.VMEM((HEADS, 2048, 3 * HD), BF16),
            dma((4,)),
            pltpu.VMEM((N, HEADS, TILES, 128), F32),
            pltpu.VMEM((HEADS, TOK, 4 * HD), BF16),
            pltpu.VMEM((N, HEADS * TILES, 128), BF16),
            pltpu.VMEM((N, HEADS * TILES, 128), BF16),
            pltpu.VMEM((HEADS, 1, SLOTS), F32),
            pltpu.VMEM((HEADS, SLOTS, 128), F32),
            pltpu.VMEM((HEADS, TOK, 128), F32),
            pltpu.VMEM((BLK, SLOTS), BF16),
            pltpu.VMEM((HEADS, N, CAP, 4 * HD), BF16),
            pltpu.VMEM((HEADS, N, CAP, 4 * HD), BF16),
            pltpu.VMEM((W, 4 * HD), BF16),
            pltpu.VMEM((W, 3 * HD), BF16),
            pltpu.VMEM((W, HD), F32),
            pltpu.VMEM((W, HD), F32),
            pltpu.VMEM((W // BLK, BLK, BLK), F32),
            pltpu.VMEM((W // BLK, BLK, BLK), F32),
            pltpu.VMEM((HD, W), BF16),
            pltpu.VMEM((HEADS, N, CAP, 3 * HD), BF16),
            pltpu.VMEM((HEADS, N, CAP, 3 * HD), BF16),
            pltpu.VMEM((2 * NY, TOK, 256), F32),
            pltpu.VMEM((TOK, 3 * HD), F32),
            pltpu.VMEM((TOK, 3 * HD), BF16),
            pltpu.VMEM((TOK, 256), F32),
            pltpu.VMEM((NY, TOK, 256), BF16),
            pltpu.VMEM((NY, TOK, 256), BF16),
            pltpu.VMEM((3, TOK, 256), BF16),
            pltpu.VMEM((2, HALF, 256), BF16),
            pltpu.VMEM((2, HALF, 256), BF16),
            pltpu.VMEM((2, HALF, 256), BF16),
            pltpu.VMEM((2, HALF, 256), BF16),
            dma((1,)), dma((LEVELS,)),
            dma((HEADS,)), dma((HEADS,)),
            dma((HEADS,)), dma((HEADS, LEVELS)),
            dma((2, HEADS)),
            dma((1,)), dma((NY, 2)),
            dma((1,)), dma((2,)),
            dma((1,)), dma((2,)),
            dma((1,)), dma((2,)),
        ],
        compiler_params=pltpu.CompilerParams(
            collective_id=0, has_side_effects=True, vmem_limit_bytes=60 * 1024 * 1024
        ),
    )(queries, keys, values, out_grad, members, centroids, proj_weight)
    return pl.pallas_call(
        hand_over,
        out_shape=(
            jax.ShapeDtypeStruct((TOK, HEADS * HD), BF16),
            jax.ShapeDtypeStruct((HEADS, 1, HD), F32),
        ),
        in_specs=[vmem] * 2,
        out_specs=(vmem, vmem),
    )(*results)


def solution(mesh):
    return jax.shard_map(
        shards,
        mesh=mesh,
        in_specs=(
            P("seq", "head"),
            P("seq", "head"),
            P("seq", "head"),
            P("seq", "head"),
            P("head", "seq", None),
            P("head", "seq", None),
            P(None, None, "head"),
        ),
        out_specs=(P("seq", "head"), P("head", "seq", None)),
        check_vma=False,
    )
```

```python
import math

import jax
import jax.numpy as jnp
from jax import lax
from jax.experimental import pallas as pl
from jax.experimental.pallas import tpu as pltpu
from jax.sharding import PartitionSpec as P

MESH = pl.DeviceIdType.MESH
F32 = jnp.float32
BF16 = jnp.bfloat16

decay_rate = 0.99

N = 32
NZ, NX = 8, 4
NY = 4
TOK = 1024
W = 1024
CAP = 64
HD = 128
HEADS = 2
SLOTS = N * CAP
GROUP = 4
BLK = 256
HALF = TOK // 2
TILES = TOK // 128
LEVELS = NZ // 2
SELF_STEP = 1


def one_hot(mask):
    return jnp.where(mask, 1.0, 0.0).astype(BF16)


def iota(shape, dim):
    return lax.broadcasted_iota(jnp.int32, shape, dim).astype(F32)


def dot_nt(a, b):
    return lax.dot_general(a, b, (((1,), (1,)), ((), ())), preferred_element_type=F32)


def dot_nn(a, b):
    return jnp.dot(a, b, preferred_element_type=F32)


def kernel(
    q_hbm, k_hbm, v_hbm, g_hbm, mem_hbm, cent_hbm, w_hbm,
    out_ref, newc_ref,
    mem_ref, cent_ref, w_ref, in_sem, codes_w, tab, codes_s, codes_r, destrow, dest_t, slot_t, hot,
    stage_f, recv_f, x_ref, y_ref, dk_ref, dv_ref, p_scr, d_scr, k_t,
    stage_r, recv_r, first, z_sum, z_ref, own, part, part_r, p2, hop_r, hop_s, dir_r, last_r,
    code_ss, code_rs, fwd_ss, fwd_rs, ret_ss, ret_rs, self_sem,
    core_ss, core_rs, hop_ss, hop_rs, dir_ss, dir_rs, last_ss, last_rs,
):
    me = lax.axis_index("seq")
    hd = lax.axis_index("head")
    my_z, my_x = lax.div(me, NX), lax.rem(me, NX)
    my_y, core = lax.div(hd, 2), lax.rem(hd, 2)
    sibling = my_y * 2 + (1 - core)
    y_next = lax.rem(my_y + 1, NY)
    y_prev = lax.rem(my_y + NY - 1, NY)
    y_far = lax.rem(my_y + 2, NY)
    next_hd = y_next * 2 + core
    prev_hd = y_prev * 2 + core

    def level_z(level, side):
        dz = jnp.where(side == 0, NZ // 2 - level, jnp.where(level == 0, 0, NZ // 2 + level))
        return lax.rem(my_z + dz, NZ)

    def peer(n):
        in_level = lax.rem(n, 2 * NX)
        dx = lax.div(in_level, 2)
        return level_z(lax.div(n, 2 * NX), lax.rem(in_level, 2)) * NX + lax.rem(my_x + dx, NX)

    barrier = pltpu.get_barrier_semaphore()

    def greet(n, carry):
        @pl.when(n != SELF_STEP)
        def _():
            pl.semaphore_signal(barrier, inc=1, device_id=(peer(n), hd), device_id_type=MESH)
        return carry

    lax.fori_loop(0, N, greet, 0)
    for other in (sibling, next_hd, prev_hd):
        pl.semaphore_signal(barrier, inc=1, device_id=(me, other), device_id_type=MESH)

    mem_in = pltpu.make_async_copy(mem_hbm, mem_ref, in_sem.at[0])
    mem_in.start()
    cent_in = pltpu.make_async_copy(cent_hbm, cent_ref, in_sem.at[1])
    cent_in.start()
    for h in range(HEADS):
        for at, ref in enumerate((q_hbm, k_hbm, v_hbm, g_hbm)):
            pltpu.make_async_copy(
                ref.at[:, h * HD : (h + 1) * HD], tab.at[h, :, at * HD : (at + 1) * HD], in_sem.at[2]
            ).start()
    for h in range(HEADS):
        for a in range(3):
            pltpu.make_async_copy(
                w_hbm.at[a, :, h * HD : (h + 1) * HD], w_ref.at[h, :, a * HD : (a + 1) * HD], in_sem.at[3]
            ).start()
    mem_in.wait()

    runs = []
    for h in range(HEADS):
        m = mem_ref[h]
        dev = lax.broadcasted_iota(jnp.int32, (N, W), 0)
        eq = (m >> 10) == dev
        start = jnp.sum(jnp.where((m >> 10) < dev, 1.0, 0.0), axis=1, keepdims=True)
        count = jnp.sum(jnp.where(eq, 1.0, 0.0), axis=1, keepdims=True)
        start_of = jnp.sum(jnp.where(eq, start, 0.0), axis=0, keepdims=True)
        rank = iota((1, W), 1) + 1.0 - start_of
        runs.append((start, count))
        ranks = jnp.where(
            (m >> 7) == lax.broadcasted_iota(jnp.int32, (N * TILES, W), 0), rank, 0.0
        ).astype(BF16)
        low = one_hot((m & 127) == lax.broadcasted_iota(jnp.int32, (128, W), 0))
        codes_w[:, h] = dot_nt(ranks, low).reshape(N, TILES, 128)
    codes_s[...] = codes_w[...].reshape(N, HEADS * TILES, 128).astype(BF16)

    pl.semaphore_wait(barrier, N - 1 + 3)

    def code_copy(src, dst, step, other):
        return pltpu.make_async_remote_copy(
            src_ref=src, dst_ref=dst, send_sem=code_ss.at[0], recv_sem=code_rs.at[step],
            device_id=(other, hd), device_id_type=MESH,
        )

    def send_codes(n, carry):
        @pl.when(n != SELF_STEP)
        def _():
            to = peer(n)
            code_copy(codes_s.at[to], codes_r.at[me], lax.div(n, 2 * NX), to).start()
        return carry

    def wait_codes(step, count):
        some = pl.ds(0, count)
        code_copy(codes_s.at[some], codes_r.at[some], step, me).wait_recv()

    lax.fori_loop(0, N, send_codes, 0)
    codes_r[me] = codes_s[me]

    for h in range(HEADS):
        start, count = runs[h]
        slot = lax.broadcasted_iota(jnp.int32, (N, SLOTS), 1)
        dev2 = lax.broadcasted_iota(jnp.int32, (N, SLOTS), 0)
        rank_at = (slot & (CAP - 1)).astype(F32)
        place = jnp.where(rank_at < count, start + rank_at, -1.0)
        destrow[h] = jnp.sum(jnp.where((slot >> 6) == dev2, place, 0.0), axis=0, keepdims=True)
    pltpu.make_async_copy(tab, tab, in_sem.at[2]).wait()

    def fwd_copy(h, src, dst, other):
        return pltpu.make_async_remote_copy(
            src_ref=stage_f.at[h, src], dst_ref=recv_f.at[h, dst],
            send_sem=fwd_ss.at[h], recv_sem=fwd_rs.at[h],
            device_id=(other, hd), device_id_type=MESH,
        )

    def ret_copy(h, src, dst, other, step):
        return pltpu.make_async_remote_copy(
            src_ref=stage_r.at[h, src], dst_ref=recv_r.at[h, dst],
            send_sem=ret_ss.at[h, step], recv_sem=ret_rs.at[h, step],
            device_id=(other, hd), device_id_type=MESH,
        )

    def fwd_self(h):
        return pltpu.make_async_copy(stage_f.at[h, SELF_STEP], recv_f.at[h, me], self_sem.at[0, h])

    def ret_self(h):
        return pltpu.make_async_copy(stage_r.at[h, SELF_STEP], recv_r.at[h, me], self_sem.at[1, h])

    def launch(gi, copy_of, self_copy):
        for u in range(GROUP):
            n = gi * GROUP + u
            to = peer(n)

            @pl.when(n != SELF_STEP)
            def _():
                copy_of(n, to).start()

            @pl.when(n == SELF_STEP)
            def _():
                self_copy.start()

    others = pl.ds(0, N - 1)

    def sent_ret(h, step):
        some = pl.ds(0, 2 * NX - (step == 0))
        ret_copy(h, some, some, me, step).wait_send()

    def wait_ret(h, step):
        some = pl.ds(0, 2 * NX - (step == 0))
        ret_copy(h, some, some, me, step).wait_recv()
        if step == 0:
            ret_self(h).wait()

    rank_rows = iota((CAP, 128), 0) + 1.0
    lanes = iota((CAP, 128), 1)

    def gather_head(h, carry):
        def group(gi, inner):
            @pl.when((h == 0) & (gi == 0))
            def _():
                wait_codes(0, 2 * NX - 1)

            @pl.when((h == 0) & (gi > 0) & (lax.rem(gi, 2) == 0))
            def _():
                wait_codes(lax.div(gi, 2), 2 * NX)

            for u in range(GROUP):
                to = peer(gi * GROUP + u)

                @pl.when(h == 0)
                def _():
                    codes_w[to] = codes_r[to].astype(F32).reshape(HEADS, TILES, 128)

                for tc in range(TILES):
                    row = codes_w[to, h, tc : tc + 1, :]
                    hot[u * CAP : (u + 1) * CAP, tc * 128 : (tc + 1) * 128] = one_hot(row == rank_rows)
            rows = dot_nn(hot[:, :TOK], tab[h])
            stage_f[h, pl.ds(gi * GROUP, GROUP)] = rows.astype(BF16).reshape(GROUP, CAP, 4 * HD)
            launch(gi, lambda n, to: fwd_copy(h, n, me, to), fwd_self(h))
            return inner

        return lax.fori_loop(0, N // GROUP, group, carry)

    lax.fori_loop(0, HEADS, gather_head, 0)

    for h in range(HEADS):
        dest_t[h] = jnp.transpose(jnp.broadcast_to(destrow[h], (128, SLOTS)))
    for h in range(HEADS):
        slot = jnp.zeros((TILES, 128), F32)
        for c in range(N):
            code = codes_w[c, h]
            slot = slot + jnp.where(code > 0.0, code + (c * CAP - 1.0), 0.0)
        for tc in range(TILES):
            slot_t[h, tc * 128 : (tc + 1) * 128, :] = jnp.transpose(
                jnp.broadcast_to(slot[tc : tc + 1, :], (128, 128))
            )

    exp_scale = math.log2(math.e) / math.sqrt(HD)
    scale = 1.0 / math.sqrt(HD)
    causal = lax.broadcasted_iota(jnp.int32, (BLK, BLK), 0) <= lax.broadcasted_iota(
        jnp.int32, (BLK, BLK), 1
    )

    cent_in.wait()

    def cluster_head(h, carry):
        fwd_copy(h, others, others, me).wait_recv()
        fwd_self(h).wait()

        def order(ib, sums):
            place = iota((BLK, 128), 0) + (ib * BLK).astype(F32)
            for pc in range(SLOTS // 128):
                row = destrow[h, :, pc * 128 : (pc + 1) * 128]
                hot[:, pc * 128 : (pc + 1) * 128] = one_hot(row == place)
            rows = dot_nn(hot[...], recv_f[h].reshape(SLOTS, 4 * HD))
            x_ref[pl.ds(ib * BLK, BLK), :] = rows.astype(BF16)
            return sums + jnp.sum(rows[:, :HD] + rows[:, HD : 2 * HD], axis=0, keepdims=True)

        sums = lax.fori_loop(0, W // BLK, order, jnp.zeros((1, HD), F32))
        newc_ref[h] = decay_rate * cent_ref[h] + 0.5 * (1.0 - decay_rate) * sums

        k_t[...] = jnp.transpose(x_ref[:, HD : 2 * HD].astype(F32)).astype(BF16)

        for b in range(W // BLK):
            low = b * BLK
            q_b = x_ref[low : low + BLK, 0:HD]
            g_b = x_ref[low : low + BLK, 3 * HD : 4 * HD]
            top = None
            for jb in range(b + 1):
                s = dot_nt(x_ref[jb * BLK : (jb + 1) * BLK, HD : 2 * HD], q_b)
                if jb == b:
                    s = jnp.where(causal, s, -jnp.inf)
                p_scr[jb] = s
                part_top = jnp.max(s, axis=0, keepdims=True)
                top = part_top if top is None else jnp.maximum(top, part_top)
            total = jnp.zeros((1, BLK), F32)
            delta = jnp.zeros((1, BLK), F32)
            for jb in range(b + 1):
                p = jnp.exp2((p_scr[jb] - top) * exp_scale)
                d = dot_nt(x_ref[jb * BLK : (jb + 1) * BLK, 2 * HD : 3 * HD], g_b)
                p_scr[jb] = p
                d_scr[jb] = d
                total = total + jnp.sum(p, axis=0, keepdims=True)
                delta = delta + jnp.sum(p * d, axis=0, keepdims=True)
            inv = 1.0 / total
            delta = delta * inv
            dq_t = jnp.zeros((HD, BLK), F32)
            for jb in range(b + 1):
                rows = slice(jb * BLK, (jb + 1) * BLK)
                p = p_scr[jb] * inv
                p_low = p.astype(BF16)
                ds = (p * (d_scr[jb] - delta)).astype(BF16)
                dv = dot_nn(p_low, g_b)
                dk = dot_nn(ds, q_b)
                dq_t = dq_t + dot_nn(k_t[:, rows], ds)
                if jb == b:
                    dv_ref[rows, :] = dv
                    dk_ref[rows, :] = dk
                else:
                    dv_ref[rows, :] += dv
                    dk_ref[rows, :] += dk
            y_ref[low : low + BLK, 0:HD] = (jnp.transpose(dq_t) * scale).astype(BF16)
        y_ref[:, HD : 2 * HD] = (dk_ref[...] * scale).astype(BF16)
        y_ref[:, 2 * HD : 3 * HD] = dv_ref[...].astype(BF16)

        def group(gi, inner):
            for u in range(GROUP):
                to = peer(gi * GROUP + u)
                place = dest_t[h, pl.ds(pl.multiple_of(to * CAP, CAP), CAP), :]
                for ic in range(W // 128):
                    hot[u * CAP : (u + 1) * CAP, ic * 128 : (ic + 1) * 128] = one_hot(
                        place == lanes + ic * 128.0
                    )
            rows = dot_nn(hot[:, :W], y_ref[...])
            stage_r[h, pl.ds(gi * GROUP, GROUP)] = rows.astype(BF16).reshape(GROUP, CAP, 3 * HD)

            @pl.when((h == HEADS - 1) & (gi == 2 * (LEVELS - 1)))
            def _():
                sent_ret(HEADS - 1, 0)

            launch(gi, lambda n, to: ret_copy(h, n, me, to, lax.div(gi, 2)), ret_self(h))
            return inner

        return lax.fori_loop(0, N // GROUP, group, carry)

    lax.fori_loop(0, HEADS, cluster_head, 0)

    for h in range(HEADS):
        fwd_copy(h, others, others, me).wait_send()
    pltpu.make_async_copy(w_ref, w_ref, in_sem.at[3]).wait()

    wide = iota((BLK, 128), 1)

    def put_hot(h, tb, carry):
        rows_at = pl.ds(pl.multiple_of(tb * BLK, BLK), BLK)
        place = slot_t[h, rows_at, :]
        for pc in range(SLOTS // 128):
            part_at, lane = divmod(pc * 128, 4 * HD)
            block = one_hot(place == wide + pc * 128.0).reshape(BLK // CAP, CAP, 128)
            some = pl.ds(part_at % 2 * (TOK // CAP) + tb * (BLK // CAP), BLK // CAP)
            stage_f[part_at // 2, some, :, lane : lane + 128] = block
        return carry

    def tokens(h, tb):
        acc = None
        for part_at in range(SLOTS // (4 * HD)):
            some = pl.ds(part_at % 2 * (TOK // CAP) + tb * (BLK // CAP), BLK // CAP)
            hots = stage_f[part_at // 2, some].reshape(BLK, 4 * HD)
            runs_at = 4 * HD // CAP
            rows = recv_r[h, part_at * runs_at : (part_at + 1) * runs_at].reshape(4 * HD, 3 * HD)
            term = dot_nn(hots, rows)
            acc = term if acc is None else acc + term
        return acc.astype(BF16)

    def tokens_step(step):
        for half in range(2):
            term = None
            for side in range(2):
                at_z = level_z(step, side)
                lane = pl.ds(pl.multiple_of(lax.rem(at_z, 2) * (NX * CAP), NX * CAP), NX * CAP)
                rows = recv_r[1, pl.ds(at_z * NX, NX)].reshape(NX * CAP, 3 * HD)
                low = lax.rem(lax.div(at_z, 2), 2) * (TOK // CAP) + half * (HALF // CAP)
                hots = stage_f[lax.div(at_z, 4), pl.ds(low, HALF // CAP), :, lane].reshape(HALF, NX * CAP)
                more = dot_nn(hots, rows)
                term = more if term is None else term + more
            at = slice(half * HALF, (half + 1) * HALF)
            if step == 0:
                z_sum[at, :] = term
            elif step < LEVELS - 1:
                z_sum[at, :] += term
            else:
                z_ref[at, :] = (z_sum[at, :] + term).astype(BF16)

    lax.fori_loop(0, TOK // BLK, lambda tb, c: put_hot(0, tb, c), 0)
    for step in range(LEVELS):
        wait_ret(0, step)

    def first_part(tb, carry):
        z = tokens(0, tb)
        rows_at = pl.ds(pl.multiple_of(tb * BLK, BLK), BLK)

        def one(d, inner):
            w_d = w_ref[0, pl.ds(pl.multiple_of(d * 256, 256), 256), :]
            first[d, rows_at, :] = dot_nt(z, w_d)
            return inner

        return lax.fori_loop(0, 2 * NY, one, carry)

    lax.fori_loop(0, TOK // BLK, first_part, 0)
    lax.fori_loop(0, TOK // BLK, lambda tb, c: put_hot(1, tb, c), 0)
    for step in range(LEVELS):
        wait_ret(1, step)
        tokens_step(step)

    def y_copy(src, dst, send_sem, recv_sem, other):
        return pltpu.make_async_remote_copy(
            src_ref=src, dst_ref=dst, send_sem=send_sem, recv_sem=recv_sem,
            device_id=(me, other), device_id_type=MESH,
        )

    blocks = (y_far, y_next, y_prev, my_y)
    halves = (slice(0, HALF), slice(HALF, TOK))

    def core_copy(r, f):
        return y_copy(
            part.at[r, halves[f]], part_r.at[r, halves[f]], core_ss.at[0], core_rs.at[r, f], sibling
        )

    def hop_copy(f):
        return y_copy(
            p2.at[0, halves[f]], hop_r.at[f], hop_ss.at[0], hop_rs.at[f], (next_hd, prev_hd)[f]
        )

    def dir_copy(f):
        return y_copy(
            p2.at[2 - f, halves[f]], dir_r.at[f], dir_ss.at[0], dir_rs.at[f], (prev_hd, next_hd)[f]
        )

    def last_copy(f):
        return y_copy(hop_s.at[f], last_r.at[f], last_ss.at[0], last_rs.at[f], (next_hd, prev_hd)[f])

    def block(r, side, half):
        d = blocks[r] * 2 + side
        w_d = w_ref[1, pl.ds(pl.multiple_of(d * 256, 256), 256), :]
        return first[d, half, :] + dot_nt(z_ref[half, :], w_d)

    def theirs(r):
        for f in range(2):
            part[r, halves[f], :] = block(r, 1 - core, halves[f]).astype(BF16)
            core_copy(r, f).start()

    def ours(r):
        for half in halves:
            own[half, :] = block(r, core, half)

    def merge(r, f):
        core_copy(r, f).wait_recv()
        half = halves[f]
        p2[r, half, :] = (own[half, :] + part_r[r, half, :].astype(F32)).astype(BF16)

    def relay(f):
        hop_copy(f).wait_recv()
        hop_s[f] = (hop_r[f].astype(F32) + p2[1 + f, halves[f], :].astype(F32)).astype(BF16)
        last_copy(f).start()

    theirs(0)
    ours(0)
    theirs(1)
    for f in range(2):
        merge(0, f)
        hop_copy(f).start()
    theirs(2)
    ours(1)
    merge(1, 1)
    dir_copy(1).start()
    merge(1, 0)
    ours(2)
    merge(2, 0)
    dir_copy(0).start()
    merge(2, 1)
    theirs(3)
    relay(0)
    relay(1)
    ours(3)
    for f in range(2):
        core_copy(3, f).wait_recv()
        own[halves[f], :] += part_r[3, halves[f], :].astype(F32)
    for f in range(2):
        dir_copy(f).wait_recv()
        own[halves[f], :] += dir_r[f].astype(F32)
    for f in range(2):
        last_copy(f).wait_recv()
        out_ref[halves[f], :] = (own[halves[f], :] + last_r[f].astype(F32)).astype(BF16)

    code_copy(codes_s.at[others], codes_r.at[others], 0, me).wait_send()
    for h in range(HEADS):
        for step in range(LEVELS):
            if (h, step) != (HEADS - 1, 0):
                sent_ret(h, step)
    y_copy(part, part_r, core_ss.at[0], core_rs.at[0, 0], sibling).wait_send()
    for sem in (hop_ss, dir_ss, last_ss):
        y_copy(hop_s, hop_r, sem.at[0], hop_rs.at[0], next_hd).wait_send()


def hand_over(grad_ref, cent_ref, out_ref, newc_ref):
    out_ref[...] = grad_ref[...]
    newc_ref[...] = cent_ref[...]


def shards(queries, keys, values, out_grad, members, centroids, proj_weight):
    vmem = pl.BlockSpec(memory_space=pltpu.VMEM)
    dma = pltpu.SemaphoreType.DMA
    results = pl.pallas_call(
        kernel,
        out_shape=(
            jax.ShapeDtypeStruct((TOK, HEADS * HD), BF16),
            jax.ShapeDtypeStruct((HEADS, 1, HD), F32),
        ),
        in_specs=[pl.BlockSpec(memory_space=pl.ANY)] * 7,
        out_specs=(vmem, vmem),
        scratch_shapes=[
            pltpu.VMEM((HEADS, 1, W), jnp.int32),
            pltpu.VMEM((HEADS, 1, HD), F32),
            pltpu.VMEM((HEADS, 2048, 3 * HD), BF16),
            dma((4,)),
            pltpu.VMEM((N, HEADS, TILES, 128), F32),
            pltpu.VMEM((HEADS, TOK, 4 * HD), BF16),
            pltpu.VMEM((N, HEADS * TILES, 128), BF16),
            pltpu.VMEM((N, HEADS * TILES, 128), BF16),
            pltpu.VMEM((HEADS, 1, SLOTS), F32),
            pltpu.VMEM((HEADS, SLOTS, 128), F32),
            pltpu.VMEM((HEADS, TOK, 128), F32),
            pltpu.VMEM((BLK, SLOTS), BF16),
            pltpu.VMEM((HEADS, N, CAP, 4 * HD), BF16),
            pltpu.VMEM((HEADS, N, CAP, 4 * HD), BF16),
            pltpu.VMEM((W, 4 * HD), BF16),
            pltpu.VMEM((W, 3 * HD), BF16),
            pltpu.VMEM((W, HD), F32),
            pltpu.VMEM((W, HD), F32),
            pltpu.VMEM((W // BLK, BLK, BLK), F32),
            pltpu.VMEM((W // BLK, BLK, BLK), F32),
            pltpu.VMEM((HD, W), BF16),
            pltpu.VMEM((HEADS, N, CAP, 3 * HD), BF16),
            pltpu.VMEM((HEADS, N, CAP, 3 * HD), BF16),
            pltpu.VMEM((2 * NY, TOK, 256), F32),
            pltpu.VMEM((TOK, 3 * HD), F32),
            pltpu.VMEM((TOK, 3 * HD), BF16),
            pltpu.VMEM((TOK, 256), F32),
            pltpu.VMEM((NY, TOK, 256), BF16),
            pltpu.VMEM((NY, TOK, 256), BF16),
            pltpu.VMEM((3, TOK, 256), BF16),
            pltpu.VMEM((2, HALF, 256), BF16),
            pltpu.VMEM((2, HALF, 256), BF16),
            pltpu.VMEM((2, HALF, 256), BF16),
            pltpu.VMEM((2, HALF, 256), BF16),
            dma((1,)), dma((LEVELS,)),
            dma((HEADS,)), dma((HEADS,)),
            dma((HEADS, LEVELS)), dma((HEADS, LEVELS)),
            dma((2, HEADS)),
            dma((1,)), dma((NY, 2)),
            dma((1,)), dma((2,)),
            dma((1,)), dma((2,)),
            dma((1,)), dma((2,)),
        ],
        compiler_params=pltpu.CompilerParams(
            collective_id=0, has_side_effects=True, vmem_limit_bytes=60 * 1024 * 1024
        ),
    )(queries, keys, values, out_grad, members, centroids, proj_weight)
    return pl.pallas_call(
        hand_over,
        out_shape=(
            jax.ShapeDtypeStruct((TOK, HEADS * HD), BF16),
            jax.ShapeDtypeStruct((HEADS, 1, HD), F32),
        ),
        in_specs=[vmem] * 2,
        out_specs=(vmem, vmem),
    )(*results)


def solution(mesh):
    return jax.shard_map(
        shards,
        mesh=mesh,
        in_specs=(
            P("seq", "head"),
            P("seq", "head"),
            P("seq", "head"),
            P("seq", "head"),
            P("head", "seq", None),
            P("head", "seq", None),
            P(None, None, "head"),
        ),
        out_specs=(P("seq", "head"), P("head", "seq", None)),
        check_vma=False,
    )
```

```python
import math

import jax
import jax.numpy as jnp
from jax import lax
from jax.experimental import pallas as pl
from jax.experimental.pallas import tpu as pltpu
from jax.sharding import PartitionSpec as P

MESH = pl.DeviceIdType.MESH
F32 = jnp.float32
BF16 = jnp.bfloat16

decay_rate = 0.99

N = 32
NZ, NX = 8, 4
NY = 4
TOK = 1024
W = 1024
CAP = 64
HD = 128
HEADS = 2
SLOTS = N * CAP
GROUP = 4
BLK = 256
HALF = TOK // 2
TILES = TOK // 128
LEVELS = NZ // 2
SELF_STEP = 1


def one_hot(mask):
    return jnp.where(mask, 1.0, 0.0).astype(BF16)


def iota(shape, dim):
    return lax.broadcasted_iota(jnp.int32, shape, dim).astype(F32)


def dot_nt(a, b):
    return lax.dot_general(a, b, (((1,), (1,)), ((), ())), preferred_element_type=F32)


def dot_nn(a, b):
    return jnp.dot(a, b, preferred_element_type=F32)


def kernel(
    q_hbm, k_hbm, v_hbm, g_hbm, mem_hbm, cent_hbm, w_hbm,
    out_ref, newc_ref,
    mem_ref, cent_ref, w_ref, in_sem, codes_w, tab, codes_s, codes_r, destrow, dest_t, slot_t, hot,
    stage_f, recv_f, x_ref, y_ref, dk_ref, dv_ref, p_scr, d_scr, k_t,
    stage_r, recv_r, first, z_sum, z_ref, own, part, part_r, p2, hop_r, hop_s, dir_r, last_r,
    code_ss, code_rs, fwd_ss, fwd_rs, ret_ss, ret_rs, self_sem,
    core_ss, core_rs, hop_ss, hop_rs, dir_ss, dir_rs, last_ss, last_rs,
):
    me = lax.axis_index("seq")
    hd = lax.axis_index("head")
    my_z, my_x = lax.div(me, NX), lax.rem(me, NX)
    my_y, core = lax.div(hd, 2), lax.rem(hd, 2)
    sibling = my_y * 2 + (1 - core)
    y_next = lax.rem(my_y + 1, NY)
    y_prev = lax.rem(my_y + NY - 1, NY)
    y_far = lax.rem(my_y + 2, NY)
    next_hd = y_next * 2 + core
    prev_hd = y_prev * 2 + core

    def level_z(level, side):
        dz = jnp.where(side == 0, NZ // 2 - level, jnp.where(level == 0, 0, NZ // 2 + level))
        return lax.rem(my_z + dz, NZ)

    def peer(n):
        in_level = lax.rem(n, 2 * NX)
        dx = lax.div(in_level, 2)
        return level_z(lax.div(n, 2 * NX), lax.rem(in_level, 2)) * NX + lax.rem(my_x + dx, NX)

    barrier = pltpu.get_barrier_semaphore()

    mem_in = pltpu.make_async_copy(mem_hbm, mem_ref, in_sem.at[0])
    mem_in.start()
    rings = [(lax.rem(my_z + dz, NZ) * NX, LEVELS - min(dz, NZ - dz) if dz else 0) for dz in range(NZ)]
    across = [lax.rem(my_x + dx, NX) for dx in range(NX)]
    far_first = (4, 3, 5, 2, 6, 1, 7, 0)
    peers = [
        (rings[dz][0] + across[dx], rings[dz][1]) for dz in far_first for dx in range(NX) if dz or dx
    ]
    for to, _ in peers:
        pl.semaphore_signal(barrier, inc=1, device_id=(to, hd), device_id_type=MESH)
    for other in (sibling, next_hd, prev_hd):
        pl.semaphore_signal(barrier, inc=1, device_id=(me, other), device_id_type=MESH)

    cent_in = pltpu.make_async_copy(cent_hbm, cent_ref, in_sem.at[1])
    cent_in.start()
    for h in range(HEADS):
        for at, ref in enumerate((q_hbm, k_hbm, v_hbm, g_hbm)):
            pltpu.make_async_copy(
                ref.at[:, h * HD : (h + 1) * HD], tab.at[h, :, at * HD : (at + 1) * HD], in_sem.at[2]
            ).start()
    for h in range(HEADS):
        for a in range(3):
            pltpu.make_async_copy(
                w_hbm.at[a, :, h * HD : (h + 1) * HD], w_ref.at[h, :, a * HD : (a + 1) * HD], in_sem.at[3]
            ).start()
    mem_in.wait()

    runs = []
    for h in range(HEADS):
        m = mem_ref[h]
        dev = lax.broadcasted_iota(jnp.int32, (N, W), 0)
        eq = (m >> 10) == dev
        start = jnp.sum(jnp.where((m >> 10) < dev, 1.0, 0.0), axis=1, keepdims=True)
        count = jnp.sum(jnp.where(eq, 1.0, 0.0), axis=1, keepdims=True)
        start_of = jnp.sum(jnp.where(eq, start, 0.0), axis=0, keepdims=True)
        rank = iota((1, W), 1) + 1.0 - start_of
        runs.append((start, count))
        ranks = jnp.where(
            (m >> 7) == lax.broadcasted_iota(jnp.int32, (N * TILES, W), 0), rank, 0.0
        ).astype(BF16)
        low = one_hot((m & 127) == lax.broadcasted_iota(jnp.int32, (128, W), 0))
        codes_w[:, h] = dot_nt(ranks, low).reshape(N, TILES, 128)
    codes_s[...] = codes_w[...].reshape(N, HEADS * TILES, 128).astype(BF16)

    pl.semaphore_wait(barrier, N - 1 + 3)

    def code_copy(src, dst, step, other):
        return pltpu.make_async_remote_copy(
            src_ref=src, dst_ref=dst, send_sem=code_ss.at[0], recv_sem=code_rs.at[step],
            device_id=(other, hd), device_id_type=MESH,
        )

    for to, level in peers:
        code_copy(codes_s.at[to], codes_r.at[me], level, to).start()

    def wait_codes(step, count):
        some = pl.ds(0, count)
        code_copy(codes_s.at[some], codes_r.at[some], step, me).wait_recv()

    codes_r[me] = codes_s[me]

    pltpu.make_async_copy(tab, tab, in_sem.at[2]).wait()

    def fwd_copy(h, src, dst, other):
        return pltpu.make_async_remote_copy(
            src_ref=stage_f.at[h, src], dst_ref=recv_f.at[h, dst],
            send_sem=fwd_ss.at[h], recv_sem=fwd_rs.at[h],
            device_id=(other, hd), device_id_type=MESH,
        )

    def ret_copy(h, src, dst, other, step):
        return pltpu.make_async_remote_copy(
            src_ref=stage_r.at[h, src], dst_ref=recv_r.at[h, dst],
            send_sem=ret_ss.at[h], recv_sem=ret_rs.at[h, step],
            device_id=(other, hd), device_id_type=MESH,
        )

    def fwd_self(h):
        return pltpu.make_async_copy(stage_f.at[h, SELF_STEP], recv_f.at[h, me], self_sem.at[0, h])

    def ret_self(h):
        return pltpu.make_async_copy(stage_r.at[h, SELF_STEP], recv_r.at[h, me], self_sem.at[1, h])

    def launch(gi, copy_of, self_copy):
        for u in range(GROUP):
            n = gi * GROUP + u
            to = peer(n)

            @pl.when(n != SELF_STEP)
            def _():
                copy_of(n, to).start()

            @pl.when(n == SELF_STEP)
            def _():
                self_copy.start()

    others = pl.ds(0, N - 1)

    def wait_ret(h, step):
        some = pl.ds(0, 2 * NX - (step == 0))
        ret_copy(h, some, some, me, step).wait_recv()
        if step == 0:
            ret_self(h).wait()

    rank_rows = iota((CAP, 128), 0) + 1.0
    lanes = iota((CAP, 128), 1)

    def gather_head(h, carry):
        def group(gi, inner):
            @pl.when((h == 0) & (gi == 0))
            def _():
                wait_codes(0, 2 * NX - 1)

            @pl.when((h == 0) & (gi > 0) & (lax.rem(gi, 2) == 0))
            def _():
                wait_codes(lax.div(gi, 2), 2 * NX)

            for u in range(GROUP):
                to = peer(gi * GROUP + u)

                @pl.when(h == 0)
                def _():
                    codes_w[to] = codes_r[to].astype(F32).reshape(HEADS, TILES, 128)

                for tc in range(TILES):
                    row = codes_w[to, h, tc : tc + 1, :]
                    hot[u * CAP : (u + 1) * CAP, tc * 128 : (tc + 1) * 128] = one_hot(row == rank_rows)
            rows = dot_nn(hot[:, :TOK], tab[h])
            stage_f[h, pl.ds(gi * GROUP, GROUP)] = rows.astype(BF16).reshape(GROUP, CAP, 4 * HD)
            launch(gi, lambda n, to: fwd_copy(h, n, me, to), fwd_self(h))
            return inner

        return lax.fori_loop(0, N // GROUP, group, carry)

    lax.fori_loop(0, HEADS, gather_head, 0)

    for h in range(HEADS):
        start, count = runs[h]
        slot = lax.broadcasted_iota(jnp.int32, (N, SLOTS), 1)
        dev2 = lax.broadcasted_iota(jnp.int32, (N, SLOTS), 0)
        rank_at = (slot & (CAP - 1)).astype(F32)
        place = jnp.where(rank_at < count, start + rank_at, -1.0)
        destrow[h] = jnp.sum(jnp.where((slot >> 6) == dev2, place, 0.0), axis=0, keepdims=True)
    for h in range(HEADS):
        dest_t[h] = jnp.transpose(jnp.broadcast_to(destrow[h], (128, SLOTS)))
    for h in range(HEADS):
        slot = jnp.zeros((TILES, 128), F32)
        for c in range(N):
            code = codes_w[c, h]
            slot = slot + jnp.where(code > 0.0, code + (c * CAP - 1.0), 0.0)
        for tc in range(TILES):
            slot_t[h, tc * 128 : (tc + 1) * 128, :] = jnp.transpose(
                jnp.broadcast_to(slot[tc : tc + 1, :], (128, 128))
            )

    exp_scale = math.log2(math.e) / math.sqrt(HD)
    scale = 1.0 / math.sqrt(HD)
    causal = lax.broadcasted_iota(jnp.int32, (BLK, BLK), 0) <= lax.broadcasted_iota(
        jnp.int32, (BLK, BLK), 1
    )

    cent_in.wait()

    def cluster_head(h, carry):
        fwd_copy(h, others, others, me).wait_recv()
        fwd_self(h).wait()

        def order(ib, sums):
            place = iota((BLK, 128), 0) + (ib * BLK).astype(F32)
            for pc in range(SLOTS // 128):
                row = destrow[h, :, pc * 128 : (pc + 1) * 128]
                hot[:, pc * 128 : (pc + 1) * 128] = one_hot(row == place)
            rows = dot_nn(hot[...], recv_f[h].reshape(SLOTS, 4 * HD))
            x_ref[pl.ds(ib * BLK, BLK), :] = rows.astype(BF16)
            return sums + jnp.sum(rows[:, :HD] + rows[:, HD : 2 * HD], axis=0, keepdims=True)

        sums = lax.fori_loop(0, W // BLK, order, jnp.zeros((1, HD), F32))
        newc_ref[h] = decay_rate * cent_ref[h] + 0.5 * (1.0 - decay_rate) * sums

        k_t[...] = jnp.transpose(x_ref[:, HD : 2 * HD].astype(F32)).astype(BF16)

        for b in range(W // BLK):
            low = b * BLK
            q_b = x_ref[low : low + BLK, 0:HD]
            g_b = x_ref[low : low + BLK, 3 * HD : 4 * HD]
            top = None
            for jb in range(b + 1):
                s = dot_nt(x_ref[jb * BLK : (jb + 1) * BLK, HD : 2 * HD], q_b)
                if jb == b:
                    s = jnp.where(causal, s, -jnp.inf)
                p_scr[jb] = s
                part_top = jnp.max(s, axis=0, keepdims=True)
                top = part_top if top is None else jnp.maximum(top, part_top)
            total = jnp.zeros((1, BLK), F32)
            delta = jnp.zeros((1, BLK), F32)
            for jb in range(b + 1):
                p = jnp.exp2((p_scr[jb] - top) * exp_scale)
                d = dot_nt(x_ref[jb * BLK : (jb + 1) * BLK, 2 * HD : 3 * HD], g_b)
                p_scr[jb] = p
                d_scr[jb] = d
                total = total + jnp.sum(p, axis=0, keepdims=True)
                delta = delta + jnp.sum(p * d, axis=0, keepdims=True)
            inv = 1.0 / total
            delta = delta * inv
            dq_t = jnp.zeros((HD, BLK), F32)
            for jb in range(b + 1):
                rows = slice(jb * BLK, (jb + 1) * BLK)
                p = p_scr[jb] * inv
                p_low = p.astype(BF16)
                ds = (p * (d_scr[jb] - delta)).astype(BF16)
                dv = dot_nn(p_low, g_b)
                dk = dot_nn(ds, q_b)
                dq_t = dq_t + dot_nn(k_t[:, rows], ds)
                if jb == b:
                    dv_ref[rows, :] = dv
                    dk_ref[rows, :] = dk
                else:
                    dv_ref[rows, :] += dv
                    dk_ref[rows, :] += dk
            y_ref[low : low + BLK, 0:HD] = (jnp.transpose(dq_t) * scale).astype(BF16)
        y_ref[:, HD : 2 * HD] = (dk_ref[...] * scale).astype(BF16)
        y_ref[:, 2 * HD : 3 * HD] = dv_ref[...].astype(BF16)

        def group(gi, inner):
            for u in range(GROUP):
                to = peer(gi * GROUP + u)
                place = dest_t[h, pl.ds(pl.multiple_of(to * CAP, CAP), CAP), :]
                for ic in range(W // 128):
                    hot[u * CAP : (u + 1) * CAP, ic * 128 : (ic + 1) * 128] = one_hot(
                        place == lanes + ic * 128.0
                    )
            rows = dot_nn(hot[:, :W], y_ref[...])
            stage_r[h, pl.ds(gi * GROUP, GROUP)] = rows.astype(BF16).reshape(GROUP, CAP, 3 * HD)
            launch(gi, lambda n, to: ret_copy(h, n, me, to, lax.div(gi, 2)), ret_self(h))
            return inner

        return lax.fori_loop(0, N // GROUP, group, carry)

    lax.fori_loop(0, HEADS, cluster_head, 0)

    for h in range(HEADS):
        fwd_copy(h, others, others, me).wait_send()
    pltpu.make_async_copy(w_ref, w_ref, in_sem.at[3]).wait()

    wide = iota((BLK, 128), 1)

    def put_hot(h, tb, carry):
        rows_at = pl.ds(pl.multiple_of(tb * BLK, BLK), BLK)
        place = slot_t[h, rows_at, :]
        for pc in range(SLOTS // 128):
            part_at, lane = divmod(pc * 128, 4 * HD)
            block = one_hot(place == wide + pc * 128.0).reshape(BLK // CAP, CAP, 128)
            some = pl.ds(part_at % 2 * (TOK // CAP) + tb * (BLK // CAP), BLK // CAP)
            stage_f[part_at // 2, some, :, lane : lane + 128] = block
        return carry

    def tokens(h, tb):
        acc = None
        for part_at in range(SLOTS // (4 * HD)):
            some = pl.ds(part_at % 2 * (TOK // CAP) + tb * (BLK // CAP), BLK // CAP)
            hots = stage_f[part_at // 2, some].reshape(BLK, 4 * HD)
            runs_at = 4 * HD // CAP
            rows = recv_r[h, part_at * runs_at : (part_at + 1) * runs_at].reshape(4 * HD, 3 * HD)
            term = dot_nn(hots, rows)
            acc = term if acc is None else acc + term
        return acc.astype(BF16)

    def tokens_step(step):
        for half in range(2):
            term = None
            for side in range(2):
                at_z = level_z(step, side)
                lane = pl.ds(pl.multiple_of(lax.rem(at_z, 2) * (NX * CAP), NX * CAP), NX * CAP)
                rows = recv_r[1, pl.ds(at_z * NX, NX)].reshape(NX * CAP, 3 * HD)
                low = lax.rem(lax.div(at_z, 2), 2) * (TOK // CAP) + half * (HALF // CAP)
                hots = stage_f[lax.div(at_z, 4), pl.ds(low, HALF // CAP), :, lane].reshape(HALF, NX * CAP)
                more = dot_nn(hots, rows)
                term = more if term is None else term + more
            at = slice(half * HALF, (half + 1) * HALF)
            if step == 0:
                z_sum[at, :] = term
            elif step < LEVELS - 1:
                z_sum[at, :] += term
            else:
                z_ref[at, :] = (z_sum[at, :] + term).astype(BF16)

    lax.fori_loop(0, TOK // BLK, lambda tb, c: put_hot(0, tb, c), 0)
    for step in range(LEVELS):
        wait_ret(0, step)

    def first_part(tb, carry):
        z = tokens(0, tb)
        rows_at = pl.ds(pl.multiple_of(tb * BLK, BLK), BLK)

        def one(d, inner):
            w_d = w_ref[0, pl.ds(pl.multiple_of(d * 256, 256), 256), :]
            first[d, rows_at, :] = dot_nt(z, w_d)
            return inner

        return lax.fori_loop(0, 2 * NY, one, carry)

    lax.fori_loop(0, TOK // BLK, first_part, 0)
    lax.fori_loop(0, TOK // BLK, lambda tb, c: put_hot(1, tb, c), 0)
    for step in range(LEVELS):
        wait_ret(1, step)
        tokens_step(step)

    def y_copy(src, dst, send_sem, recv_sem, other):
        return pltpu.make_async_remote_copy(
            src_ref=src, dst_ref=dst, send_sem=send_sem, recv_sem=recv_sem,
            device_id=(me, other), device_id_type=MESH,
        )

    blocks = (y_far, y_next, y_prev, my_y)
    halves = (slice(0, HALF), slice(HALF, TOK))

    def core_copy(r, f):
        return y_copy(
            part.at[r, halves[f]], part_r.at[r, halves[f]], core_ss.at[0], core_rs.at[r, f], sibling
        )

    def hop_copy(f):
        return y_copy(
            p2.at[0, halves[f]], hop_r.at[f], hop_ss.at[0], hop_rs.at[f], (next_hd, prev_hd)[f]
        )

    def dir_copy(f):
        return y_copy(
            p2.at[2 - f, halves[f]], dir_r.at[f], dir_ss.at[0], dir_rs.at[f], (prev_hd, next_hd)[f]
        )

    def last_copy(f):
        return y_copy(hop_s.at[f], last_r.at[f], last_ss.at[0], last_rs.at[f], (next_hd, prev_hd)[f])

    def block(r, side, half):
        d = blocks[r] * 2 + side
        w_d = w_ref[1, pl.ds(pl.multiple_of(d * 256, 256), 256), :]
        return first[d, half, :] + dot_nt(z_ref[half, :], w_d)

    def theirs(r):
        for f in range(2):
            part[r, halves[f], :] = block(r, 1 - core, halves[f]).astype(BF16)
            core_copy(r, f).start()

    def ours(r):
        for half in halves:
            own[half, :] = block(r, core, half)

    def merge(r, f):
        core_copy(r, f).wait_recv()
        half = halves[f]
        p2[r, half, :] = (own[half, :] + part_r[r, half, :].astype(F32)).astype(BF16)

    def relay(f):
        hop_copy(f).wait_recv()
        hop_s[f] = (hop_r[f].astype(F32) + p2[1 + f, halves[f], :].astype(F32)).astype(BF16)
        last_copy(f).start()

    theirs(0)
    ours(0)
    theirs(1)
    for f in range(2):
        merge(0, f)
        hop_copy(f).start()
    theirs(2)
    ours(1)
    merge(1, 1)
    dir_copy(1).start()
    merge(1, 0)
    ours(2)
    merge(2, 0)
    dir_copy(0).start()
    merge(2, 1)
    theirs(3)
    relay(0)
    relay(1)
    ours(3)
    for f in range(2):
        core_copy(3, f).wait_recv()
        own[halves[f], :] += part_r[3, halves[f], :].astype(F32)
    for f in range(2):
        dir_copy(f).wait_recv()
        own[halves[f], :] += dir_r[f].astype(F32)
    for f in range(2):
        last_copy(f).wait_recv()
        out_ref[halves[f], :] = (own[halves[f], :] + last_r[f].astype(F32)).astype(BF16)

    code_copy(codes_s.at[others], codes_r.at[others], 0, me).wait_send()
    for h in range(HEADS):
        ret_copy(h, others, others, me, 0).wait_send()
    y_copy(part, part_r, core_ss.at[0], core_rs.at[0, 0], sibling).wait_send()
    for sem in (hop_ss, dir_ss, last_ss):
        y_copy(hop_s, hop_r, sem.at[0], hop_rs.at[0], next_hd).wait_send()


def hand_over(grad_ref, cent_ref, out_ref, newc_ref):
    out_ref[...] = grad_ref[...]
    newc_ref[...] = cent_ref[...]


def shards(queries, keys, values, out_grad, members, centroids, proj_weight):
    vmem = pl.BlockSpec(memory_space=pltpu.VMEM)
    dma = pltpu.SemaphoreType.DMA
    results = pl.pallas_call(
        kernel,
        out_shape=(
            jax.ShapeDtypeStruct((TOK, HEADS * HD), BF16),
            jax.ShapeDtypeStruct((HEADS, 1, HD), F32),
        ),
        in_specs=[pl.BlockSpec(memory_space=pl.ANY)] * 7,
        out_specs=(vmem, vmem),
        scratch_shapes=[
            pltpu.VMEM((HEADS, 1, W), jnp.int32),
            pltpu.VMEM((HEADS, 1, HD), F32),
            pltpu.VMEM((HEADS, 2048, 3 * HD), BF16),
            dma((4,)),
            pltpu.VMEM((N, HEADS, TILES, 128), F32),
            pltpu.VMEM((HEADS, TOK, 4 * HD), BF16),
            pltpu.VMEM((N, HEADS * TILES, 128), BF16),
            pltpu.VMEM((N, HEADS * TILES, 128), BF16),
            pltpu.VMEM((HEADS, 1, SLOTS), F32),
            pltpu.VMEM((HEADS, SLOTS, 128), F32),
            pltpu.VMEM((HEADS, TOK, 128), F32),
            pltpu.VMEM((BLK, SLOTS), BF16),
            pltpu.VMEM((HEADS, N, CAP, 4 * HD), BF16),
            pltpu.VMEM((HEADS, N, CAP, 4 * HD), BF16),
            pltpu.VMEM((W, 4 * HD), BF16),
            pltpu.VMEM((W, 3 * HD), BF16),
            pltpu.VMEM((W, HD), F32),
            pltpu.VMEM((W, HD), F32),
            pltpu.VMEM((W // BLK, BLK, BLK), F32),
            pltpu.VMEM((W // BLK, BLK, BLK), F32),
            pltpu.VMEM((HD, W), BF16),
            pltpu.VMEM((HEADS, N, CAP, 3 * HD), BF16),
            pltpu.VMEM((HEADS, N, CAP, 3 * HD), BF16),
            pltpu.VMEM((2 * NY, TOK, 256), F32),
            pltpu.VMEM((TOK, 3 * HD), F32),
            pltpu.VMEM((TOK, 3 * HD), BF16),
            pltpu.VMEM((TOK, 256), F32),
            pltpu.VMEM((NY, TOK, 256), BF16),
            pltpu.VMEM((NY, TOK, 256), BF16),
            pltpu.VMEM((3, TOK, 256), BF16),
            pltpu.VMEM((2, HALF, 256), BF16),
            pltpu.VMEM((2, HALF, 256), BF16),
            pltpu.VMEM((2, HALF, 256), BF16),
            pltpu.VMEM((2, HALF, 256), BF16),
            dma((1,)), dma((LEVELS,)),
            dma((HEADS,)), dma((HEADS,)),
            dma((HEADS,)), dma((HEADS, LEVELS)),
            dma((2, HEADS)),
            dma((1,)), dma((NY, 2)),
            dma((1,)), dma((2,)),
            dma((1,)), dma((2,)),
            dma((1,)), dma((2,)),
        ],
        compiler_params=pltpu.CompilerParams(
            collective_id=0, has_side_effects=True, vmem_limit_bytes=60 * 1024 * 1024
        ),
    )(queries, keys, values, out_grad, members, centroids, proj_weight)
    return pl.pallas_call(
        hand_over,
        out_shape=(
            jax.ShapeDtypeStruct((TOK, HEADS * HD), BF16),
            jax.ShapeDtypeStruct((HEADS, 1, HD), F32),
        ),
        in_specs=[vmem] * 2,
        out_specs=(vmem, vmem),
    )(*results)


def solution(mesh):
    return jax.shard_map(
        shards,
        mesh=mesh,
        in_specs=(
            P("seq", "head"),
            P("seq", "head"),
            P("seq", "head"),
            P("seq", "head"),
            P("head", "seq", None),
            P("head", "seq", None),
            P(None, None, "head"),
        ),
        out_specs=(P("seq", "head"), P("head", "seq", None)),
        check_vma=False,
    )
```
